256 devices in a mesh: dp: 32 (over z, x), group: 8 (over y, core).
Axes of the slice: x: 4, y: 4, z: 8, core: 2. Of those that a mesh axis runs over, the one named last changes fastest.
Arguments:
- inputs: bfloat16 [65536, 8192], P(('dp', 'group')), may hold values from -24 to 24
- grad_values: bfloat16 [65536, 512], P(('dp', 'group')), may hold values from -6 to 6
- value_weight: bfloat16 [8192, 512], P('dp'), may hold values from -0.0625 to 0.0625
- counts: int32 [256], P(('dp', 'group')), may hold values from 32 to 256, as said below
- loss_mask: int32 [65536], P(('dp', 'group')), may hold values 0 or 1
Outputs:
- input_grad: bfloat16 [65536, 8192], P(('dp', 'group'))
- weight_grad: float32 [8192, 512], P('dp')
The draws below stay inside these ranges and needn't reach their ends.
Inputs may be any that keep to these rules, and one draw needn't show every extreme that they name: `counts`: slots of a block at or past its count hold data that must not contribute; at least one block is full in every draw.
All inputs are finite; a program needn't handle non-finite values. No bound on the sum of `loss_mask` on one device may be relied on, other than what follows from the above.
Results may differ from the reference program's by a relative error of at most 0.0049.
Values may be sent and summed in bfloat16 or wider, within the bound.
No kernel may reach another device: no remote copies, remote signals or barrier semaphores. Data moves between devices by JAX's collectives and lax.ppermute only.
A program may use at most 128 MiB of HBM per device.

```python
import jax
import jax.numpy as jnp
from jax import lax

D = 8192
TOK_DEV = 256
KV_WIDTH = 512
TOKENS = 65536
N_DP = 32
N_GROUP = 8


def draw_counts(key, part):
    key = jax.random.fold_in(key, 7)
    level_key = jax.random.fold_in(key, 1)
    jitter_key = jax.random.fold_in(key, 2)
    full_key = jax.random.fold_in(key, 3)
    number = N_DP * N_GROUP
    lowest = TOK_DEV // 8
    ceiling = jax.random.randint(level_key, (), TOK_DEV // 2, TOK_DEV + 1, dtype=jnp.int32)
    order = jnp.arange(number, dtype=jnp.int32)
    base = lowest + order * (ceiling - lowest) // max(number - 1, 1)
    jitter = jax.random.randint(jitter_key, (number,), 0, TOK_DEV // 8 + 1, dtype=jnp.int32)
    filled = jnp.minimum(base + jitter, TOK_DEV)
    full_index = jax.random.randint(full_key, (), 0, number, dtype=jnp.int32)
    filled = jnp.where(order == full_index, TOK_DEV, filled)
    return filled.astype(jnp.int32)


def set_ends(drawn, own_key, least, top_value):
    index_at = [jax.random.randint(jax.random.fold_in(own_key, axis), (), 0, length) for axis, length in enumerate(drawn.shape)]
    main_axis = drawn.shape.index(max(drawn.shape))
    beside = index_at[:main_axis] + [(index_at[main_axis] + 1) % drawn.shape[main_axis]] + index_at[main_axis + 1:]
    return drawn.at[tuple(index_at)].set(least).at[tuple(beside)].set(top_value)


def spiked(array, stream_key, source, target, shards_of, factor):
    def block_of(dim):
        return (jnp.arange(array.shape[dim]) // (array.shape[dim] // shards_of)).reshape((-1,) + (1,) * (array.ndim - 1 - dim))

    one_side = jax.random.permutation(stream_key, shards_of)[block_of(target)]
    far = (block_of(target) + shards_of // 2) % shards_of
    return jnp.where((block_of(source) == one_side) | (block_of(source) == far), factor * array, array)


def steps_of(rng, shape, shards, low, largest):
    loudness = 1.0
    for position, blocks in shards:
        draws = jax.random.uniform(jax.random.fold_in(jax.random.fold_in(rng, 6), position), (blocks,), jnp.float32, low / len(shards), largest / len(shards))
        loudness = loudness * jnp.repeat(jnp.exp(draws), shape[position] // blocks).reshape((-1,) + (1,) * (len(shape) - 1 - position))
    return loudness


def noise(rng, dims, spread, limit, split=(), kind=jnp.bfloat16):
    values = spread * jax.random.normal(rng, dims, jnp.float32)
    if split:
        values = values * steps_of(rng, dims, split, -0.22, 0.18)
    return jnp.clip(values, -limit, limit).astype(kind)


def bell_draw_with(stream_key, shape, spread, most, split, heavy, kind=jnp.bfloat16):
    drawn = spread * jax.random.normal(stream_key, shape, jnp.float32)
    if split:
        drawn = drawn * steps_of(stream_key, shape, split, -0.22, 0.18)
    return jnp.clip(spiked(drawn, jax.random.fold_in(stream_key, 3), *heavy), -most, most).astype(kind)


def setup_inputs(seed: int = 0) -> dict:
    key_of = jax.random.split(jax.random.key(seed), 6)
    inputs = bell_draw_with(key_of[0], (TOKENS, D), 1.0, 24.0, ((0, 256),), (0, 1, 256, 6.0))
    grad_values = noise(key_of[1], (TOKENS, KV_WIDTH), 1.0, 6.0, ((0, 256),))
    value_weight = noise(key_of[2], (D, KV_WIDTH), D ** -0.5, 0.0625, ((0, 32),))
    counts = draw_counts(jax.random.fold_in(key_of[5], 71), 0)
    loss_mask = set_ends((jax.random.randint(key_of[4], (TOKENS,), 0, 4) < 3).astype(jnp.int32), jax.random.fold_in(key_of[4], 1), 0, 1)
    return dict(inputs=inputs, grad_values=grad_values, value_weight=value_weight, counts=counts, loss_mask=loss_mask)


def reference(inputs, grad_values, value_weight, counts, loss_mask):
    ndevices = N_DP * N_GROUP
    total = jnp.sum(counts.astype(jnp.float32))
    factor = ndevices * counts.astype(jnp.float32) / total
    positions = jnp.arange(TOK_DEV, dtype=jnp.int32)
    live = (positions[None, :] < counts[:, None]) & (loss_mask.reshape(ndevices, TOK_DEV) > 0)
    weights = factor[:, None] * live.astype(jnp.float32)
    scaled = (grad_values.reshape(ndevices, TOK_DEV, KV_WIDTH).astype(jnp.float32) * weights[:, :, None]).astype(jnp.bfloat16)

    def backward_rows(block):
        return jnp.dot(block, value_weight.T, preferred_element_type=jnp.float32).astype(jnp.bfloat16)

    input_grad = lax.map(backward_rows, scaled).reshape(TOKENS, D)

    def accumulate(carry, pair):
        block_x, block_g = pair
        return carry + jnp.dot(block_x.T, block_g, preferred_element_type=jnp.float32), None

    summed, _ = lax.scan(accumulate, jnp.zeros((D, KV_WIDTH), jnp.float32), (inputs.reshape(ndevices, TOK_DEV, D), scaled))
    return input_grad, summed
```

```python
import functools

import jax
import jax.numpy as jnp
from jax import lax
from jax.experimental import pallas as pl
from jax.experimental.pallas import tpu as pltpu
from jax.sharding import PartitionSpec as P

NZ, NX, NY = 8, 4, 4
HALF_Z = NZ // 2
DEVICES = NZ * NX * NY * 2
F32, BF16 = jnp.float32, jnp.bfloat16
MIB = 1 << 20
ANYWHERE = pl.BlockSpec(memory_space=pl.ANY)
SMEM = pl.BlockSpec(memory_space=pltpu.SMEM)


def hop(array, move):
    pairs = []
    for z in range(NZ):
        for x in range(NX):
            for y in range(NY):
                for c in range(2):
                    tz, tx, ty, tc = move(z, x, y, c)
                    source = (z * NX + x) * NY * 2 + y * 2 + c
                    target = ((tz % NZ) * NX + tx % NX) * NY * 2 + (ty % NY) * 2 + tc
                    pairs.append((source, target))
    return lax.ppermute(array, ("dp", "group"), pairs)


def swap(array):
    return hop(array, lambda z, x, y, c: (z, x, y, 1 - c))


def nt_dot(left, right):
    return lax.dot_general(left, right, (((1,), (1,)), ((), ())), preferred_element_type=F32)


def nn_dot(left, right):
    return lax.dot_general(left, right, (((1,), (0,)), ((), ())), preferred_element_type=F32)


def params(mib):
    return pltpu.CompilerParams(vmem_limit_bytes=mib * MIB)


def whole(array):
    return pl.BlockSpec(array.shape, lambda *_: (0,) * array.ndim)


def like(array):
    return jax.ShapeDtypeStruct(array.shape, array.dtype)


def partial_kernel(place, own_n, other_n, own_t, other_t, own_x, other_x, total, s0, s1, s2a, s2b, s3, total_out, own_r, other_r):
    x, y, c = place[0], place[1], place[2]
    i = pl.program_id(0)

    @pl.when(i == 0)
    def _():
        for q in range(NY):
            quarter = lax.select(c == 0, lax.rem(y + q, NY), q)
            rows = pl.ds(pl.multiple_of(quarter * 128, 128), 128)
            own_r[q * 128 : (q + 1) * 128, :] = own_t[rows, :]
            other_r[q * 128 : (q + 1) * 128, :] = other_t[rows, :]

    def store(r, j, tile):
        if r == 2:
            @pl.when(j < 2)
            def _():
                s2a[j, i] = tile

            @pl.when(j >= 2)
            def _():
                s2b[j - 2, i] = tile
        else:
            (s0, s1, None, s3)[r][j, i] = tile

    def product(at):
        cols = pl.ds(pl.multiple_of(at * 256, 256), 256)
        return own_n[0:1, :] * nn_dot(own_r[...], own_x[:, cols]) + other_n[0:1, :] * nn_dot(
            other_r[...], other_x[:, cols]
        )

    @pl.when(c == 0)
    def _():
        for at in range(NX):
            tile = product(at).astype(BF16)
            for q in range(NY):
                store(q, at, tile[q * 128 : (q + 1) * 128])

    @pl.when(c == 1)
    def _():
        for r in range(NX):
            tile = product(lax.rem(x + r, NX)).astype(BF16)
            for q in range(NY):
                store(r, q, tile[q * 128 : (q + 1) * 128])


def partials(place, own_n, other_n, own_t, other_t, inputs, other_x, total):
    tokens = own_t.shape[1]
    jobs = (4, 4, 2, 2, 4)
    return pl.pallas_call(
        partial_kernel,
        grid_spec=pltpu.PrefetchScalarGridSpec(
            num_scalar_prefetch=1,
            grid=(HALF_Z,),
            in_specs=[
                whole(own_n),
                whole(other_n),
                whole(own_t),
                whole(other_t),
                pl.BlockSpec((tokens, NX * 256), lambda i, p: (0, p[2] * HALF_Z + i)),
                pl.BlockSpec((tokens, NX * 256), lambda i, p: (0, p[2] * HALF_Z + i)),
                ANYWHERE,
            ],
            out_specs=[pl.BlockSpec((j, HALF_Z, 128, 256), lambda i, p: (0, 0, 0, 0)) for j in jobs] + [ANYWHERE],
            scratch_shapes=[pltpu.VMEM((512, tokens), BF16)] * 2,
        ),
        out_shape=[jax.ShapeDtypeStruct((j, HALF_Z, 128, 256), BF16) for j in jobs] + [like(total)],
        input_output_aliases={7: 5},
        compiler_params=params(20),
        cost_estimate=pl.CostEstimate(flops=2 * 512 * 512 * 4096, bytes_accessed=9 << 20, transcendentals=0),
    )(place, own_n, other_n, own_t, other_t, inputs, other_x, total)


def relay_kernel(plus, minus, from_minus, from_plus, *rest):
    plus_out, minus_out = rest[len(rest) // 2 - 1 : len(rest) // 2 + 1]
    plus_out[...] = (plus[...].astype(F32) + from_minus[...].astype(F32)).astype(BF16)
    minus_out[...] = (minus[...].astype(F32) + from_plus[...].astype(F32)).astype(BF16)


def relay(plus, minus, from_minus, from_plus, *through):
    half = (2, 1, 128, 256)
    low = pl.BlockSpec(half, lambda i: (0, i, 0, 0))
    high = pl.BlockSpec(half, lambda i: (1, i, 0, 0))
    count = len(through)
    return pl.pallas_call(
        relay_kernel,
        grid=(HALF_Z,),
        in_specs=[low, high, low, low] + [ANYWHERE] * count,
        out_specs=[low, high] + [ANYWHERE] * count,
        out_shape=[like(a) for a in (plus, minus, *through)],
        input_output_aliases={0: 0, 1: 1} | {4 + k: 2 + k for k in range(count)},
        compiler_params=params(8),
        cost_estimate=pl.CostEstimate(flops=1 << 20, bytes_accessed=3 << 20, transcendentals=0),
    )(plus, minus, from_minus, from_plus, *through)


def first_sum_kernel(place, a, b, c, *rest):
    count = (len(rest) - 4) // 2
    own = lax.select(place[2] == 0, place[0], place[1])
    for r, u in enumerate(rest[count : count + 4]):
        j = lax.rem(own + r, 4)
        total = a[j, 0].astype(F32) + (b[j, 0].astype(F32) + c[j, 0].astype(F32))
        u[0] = total.astype(u.dtype)


def first_sum(place, parts, *through):
    part = pl.BlockSpec((4, 1, 128, 256), lambda i, p: (0, i, 0, 0))
    out = pl.BlockSpec((1, 128, 256), lambda i, p: (i, 0, 0))
    shape = (HALF_Z, 128, 256)
    count = len(through)
    return pl.pallas_call(
        first_sum_kernel,
        grid_spec=pltpu.PrefetchScalarGridSpec(
            num_scalar_prefetch=1,
            grid=(HALF_Z,),
            in_specs=[part] * 3 + [ANYWHERE] * count,
            out_specs=[out] * 4 + [ANYWHERE] * count,
        ),
        out_shape=[jax.ShapeDtypeStruct(shape, F32)]
        + [jax.ShapeDtypeStruct(shape, BF16)] * 3
        + [like(a) for a in through],
        input_output_aliases={4 + k: 4 + k for k in range(count)},
        compiler_params=params(8),
        cost_estimate=pl.CostEstimate(flops=1 << 20, bytes_accessed=4 << 20, transcendentals=0),
    )(place, *parts, *through)


def second_sum_kernel(place, a, b, c, d, *rest):
    count = (len(rest) - 4) // 2
    for k, v in enumerate(rest[count : count + 4]):
        j = lax.rem(place[3] + k, HALF_Z)
        total = (a[j] + b[j].astype(F32)) + (c[j].astype(F32) + d[j].astype(F32))
        v[...] = total.astype(v.dtype)


def second_sum(place, parts, *through):
    count = len(through)
    shape = jax.ShapeDtypeStruct((128, 256), BF16)
    return pl.pallas_call(
        second_sum_kernel,
        grid=(1,),
        in_specs=[SMEM] + [whole(a) for a in parts] + [ANYWHERE] * count,
        out_specs=[whole(shape)] * 4 + [ANYWHERE] * count,
        out_shape=[shape] * 4 + [like(a) for a in through],
        input_output_aliases={5 + k: 4 + k for k in range(count)},
        compiler_params=params(8),
        cost_estimate=pl.CostEstimate(flops=1 << 19, bytes_accessed=1 << 20, transcendentals=0),
    )(place, *parts, *through)


def third_sum_kernel(place, a, b, c, d, *rest):
    count = (len(rest) - 2) // 2
    for core, out in zip((place[2], 1 - place[2]), rest[count : count + 2]):
        cols = pl.ds(pl.multiple_of(core * 128, 128), 128)
        out[...] = (a[:, cols].astype(F32) + b[:, cols].astype(F32)) + (
            c[:, cols].astype(F32) + d[:, cols].astype(F32)
        )


def third_sum(place, parts, *through):
    count = len(through)
    shape = jax.ShapeDtypeStruct((128, 128), F32)
    return pl.pallas_call(
        third_sum_kernel,
        grid=(1,),
        in_specs=[SMEM] + [whole(a) for a in parts] + [ANYWHERE] * count,
        out_specs=[whole(shape)] * 2 + [ANYWHERE] * count,
        out_shape=[shape] * 2 + [like(a) for a in through],
        input_output_aliases={5 + k: 2 + k for k in range(count)},
        compiler_params=params(8),
        cost_estimate=pl.CostEstimate(flops=1 << 17, bytes_accessed=1 << 19, transcendentals=0),
    )(place, *parts, *through)


def finish_kernel(place, total, own, y1, y2, y3, other, through, out, through_out):
    y, c = place[1], place[2]
    inverse = DEVICES / total[0:1, 0:128]
    for r, mine in enumerate((own, y1, y2, y3)):
        feature = lax.rem(y + NY - r, NY)
        cols = pl.ds(pl.multiple_of(feature * 128, 128), 128)
        for core, tile in ((c, mine[...]), (1 - c, other[r])):
            rows = pl.ds(pl.multiple_of(core * 128, 128), 128)
            out[rows, cols] = (tile * inverse).T


def finish(place, total, own, gathered, other, through):
    parts = (own, *gathered, other)
    shape = jax.ShapeDtypeStruct((256, 512), F32)
    return pl.pallas_call(
        finish_kernel,
        grid=(1,),
        in_specs=[SMEM, whole(total)] + [whole(a) for a in parts] + [ANYWHERE],
        out_specs=[whole(shape), ANYWHERE],
        out_shape=[shape, like(through)],
        input_output_aliases={7: 1},
        compiler_params=params(8),
        cost_estimate=pl.CostEstimate(flops=1 << 18, bytes_accessed=1 << 20, transcendentals=0),
    )(place, total, *parts, through)


def assemble_kernel(place, own, near, near_other, far, *rest):
    x, c = place[0], place[2]
    step = 1 - 2 * c
    out = rest[2]
    out[x] = own[...]
    out[lax.rem(x - step + NX, NX)] = near[...]
    out[lax.rem(x + step + NX, NX)] = near_other[...]
    out[lax.rem(x + 2, NX)] = far[...]


def assemble(place, parts, total, dep):
    rows, width = parts[0].shape
    shape = jax.ShapeDtypeStruct((NX, rows, width), BF16)
    return pl.pallas_call(
        assemble_kernel,
        grid=(1,),
        in_specs=[SMEM] + [whole(a) for a in parts] + [ANYWHERE] * 2,
        out_specs=[whole(shape), ANYWHERE],
        out_shape=[shape, like(total)],
        input_output_aliases={5: 1},
        compiler_params=params(8),
        cost_estimate=pl.CostEstimate(flops=0, bytes_accessed=2 << 20, transcendentals=0),
    )(place, *parts, total, dep)


def project_kernel(pieces, cols, filled, total, grads, *refs):
    out = refs[-5]
    held, made, in_sems, out_sems = refs[-4:]
    span = held.shape[1]
    loads, stores = [], []
    for n, (k, start) in enumerate(pieces):
        loads.append(pltpu.make_async_copy(refs[k].at[pl.ds(start, span)], held.at[n], in_sems.at[n]))
        to = pl.ds(pl.multiple_of(cols[k] + start, 256), span)
        stores.append(pltpu.make_async_copy(made.at[n], out.at[:, to], out_sems.at[n]))
    for load in loads:
        load.start()
    scale = filled[0:1, :] * (DEVICES / total[0:1, :])
    for n, load in enumerate(loads):
        load.wait()
        for at in range(0, span, 256):
            made[n, :, at : at + 256] = (nt_dot(grads[...], held[n, at : at + 256, :]) * scale).astype(BF16)
        stores[n].start()
    for store in stores:
        store.wait()


def project(cols, filled, total, grads, chunks, out):
    tokens, width = grads.shape
    span = 512
    pieces = [(k, start) for k, chunk in enumerate(chunks) for start in range(0, chunk.shape[0], span)]
    count = len(pieces)
    operands = [cols, filled, total, grads, *chunks] + ([] if out is None else [out])
    return pl.pallas_call(
        functools.partial(project_kernel, pieces),
        grid=(1,),
        in_specs=[SMEM] + [whole(a) for a in operands[1:4]] + [ANYWHERE] * (len(operands) - 4),
        out_specs=ANYWHERE,
        out_shape=jax.ShapeDtypeStruct((tokens, NZ * NX * 256), BF16),
        scratch_shapes=[
            pltpu.VMEM((count, span, width), BF16),
            pltpu.VMEM((count, tokens, span), BF16),
            pltpu.SemaphoreType.DMA((count,)),
            pltpu.SemaphoreType.DMA((count,)),
        ],
        input_output_aliases={} if out is None else {len(operands) - 1: 0},
        compiler_params=params(24),
        cost_estimate=pl.CostEstimate(
            flops=2 * tokens * width * span * count, bytes_accessed=count * span * 1536, transcendentals=0
        ),
    )(*operands)


def local(inputs, grad_values, value_weight, counts, loss_mask):
    tok_rows = inputs.shape[0]
    dp, group = lax.axis_index("dp"), lax.axis_index("group")
    z, x, y, c = dp // NX, dp % NX, group // 2, group % 2
    place = jnp.stack([x, y, c, z]).astype(jnp.int32)
    dir_z = 1 - 2 * c

    other_x = swap(inputs)
    near = hop(value_weight, lambda z, x, y, c: (z, x + 1 - 2 * c, y, c))
    filled = jnp.full((8, 256), counts[0].astype(F32))
    other_filled = swap(filled)
    positions = jnp.arange(tok_rows, dtype=jnp.int32)
    live = (positions < counts[0]) & (loss_mask > 0)
    grads = jnp.where(live[:, None], grad_values, jnp.zeros_like(grad_values))
    own_t = grads.T
    other_t = swap(own_t)

    rows, width = value_weight.shape
    near_other = swap(near)
    far = hop(near, lambda z, x, y, c: (z, x + 1 - 2 * c, y, c))

    total = filled + hop(filled, lambda z, x, y, c: (z, x, y + 1, c))
    total = total + hop(total, lambda z, x, y, c: (z, x, y + 2, c))
    s0, s1, s2a, s2b, s3, total = partials(place, filled, other_filled, own_t, other_t, inputs, other_x, total)
    s_moves = lambda r: lambda z, x, y, c: (z, x, y + r, c) if c == 0 else (z, x + r, y, c)
    u_moves = lambda r: lambda z, x, y, c: (z, x + r, y, c) if c == 0 else (z, x, y + r, c)
    around = lambda z, x, y, c: (z + 1 - 2 * c, x, y, c)
    total = total + swap(total)
    chunk, total = assemble(place, (value_weight, near, near_other, far), total, s0)
    chunk = chunk.reshape(NX * rows, width)

    ring1 = hop(chunk, around)
    passed_plus, passed_minus = hop(s2a, s_moves(1)), hop(s2b, s_moves(-1))
    total = total + hop(total, lambda z, x, y, c: (z, x + 1, y, c))
    s1, s3, ring1, total = relay(s1, s3, passed_plus, passed_minus, ring1, total)

    ring2, ring1_other = hop(ring1, around), swap(ring1)
    first = (s0, hop(s1, s_moves(1)), hop(s3, s_moves(-1)))
    total = total + hop(total, lambda z, x, y, c: (z, x + 2, y, c))
    u0, u1, u2, u3, ring2, ring1_other, total = first_sum(place, first, ring2, ring1_other, total)

    ring3, ring2_other = hop(ring2, around), swap(ring2)
    second = [u0] + [hop(u, u_moves(r)) for r, u in ((1, u1), (2, u2), (3, u3))]
    total = total + hop(total, lambda z, x, y, c: (z + 1, x, y, c))
    *sends, ring3, ring2_other, total = second_sum(place, second, ring3, ring2_other, total)

    half = NX * rows // 2
    last = hop(lax.dynamic_slice(ring3, (c * half, 0), (half, width)), around)
    ring3_other = swap(ring3)
    third = [
        hop(sends[k], lambda z, x, y, c: (HALF_Z * c + (z + k) % HALF_Z, x, y, z // HALF_Z)) for k in range(4)
    ]
    total = total + hop(total, lambda z, x, y, c: (z + 2, x, y, c))
    kept, given, last, ring3_other, total = third_sum(place, third, last, ring3_other, total)

    def col_of(distance):
        return ((z + distance + NZ) % NZ) * (NX * rows)

    kept = kept + swap(given)
    total = total + hop(total, lambda z, x, y, c: (z + 4, x, y, c))
    last_other = swap(last)
    gathered = [hop(kept, lambda z, x, y, c: (z, x, y + r, c)) for r in range(1, 4)]
    cols = jnp.stack([col_of(0)] + [col_of(s * dir_z) for s in (-1, 1, -2, 2)]).astype(jnp.int32)
    input_grad = project(
        cols, filled, total, grads, (chunk, ring1, ring1_other, ring2, ring2_other), None
    )
    cols = jnp.stack(
        [col_of(-3 * dir_z), col_of(3 * dir_z), col_of(HALF_Z) + c * half, col_of(HALF_Z) + (1 - c) * half]
    ).astype(jnp.int32)
    input_grad = project(cols, filled, total, grads, (ring3, ring3_other, last, last_other), input_grad)
    other = swap(jnp.stack([kept, *gathered]))
    weight_grad, input_grad = finish(place, total, kept, gathered, other, input_grad)
    return (input_grad, weight_grad)


def solution(mesh):
    return jax.shard_map(
        local,
        mesh=mesh,
        in_specs=(
            P(("dp", "group"), None),
            P(("dp", "group"), None),
            P("dp", None),
            P(("dp", "group")),
            P(("dp", "group")),
        ),
        out_specs=(P(("dp", "group"), None), P("dp", None)),
        check_vma=False,
    )
```

```python
import functools

import jax
import jax.numpy as jnp
from jax import lax
from jax.experimental import pallas as pl
from jax.experimental.pallas import tpu as pltpu
from jax.sharding import PartitionSpec as P

NZ, NX, NY = 8, 4, 4
HALF_Z = NZ // 2
DEVICES = NZ * NX * NY * 2
PAD = 16
F32, BF16 = jnp.float32, jnp.bfloat16
MIB = 1 << 20
ANYWHERE = pl.BlockSpec(memory_space=pl.ANY)
HBM = pl.BlockSpec(memory_space=pltpu.HBM)
SMEM = pl.BlockSpec(memory_space=pltpu.SMEM)


def hop(array, move):
    pairs = []
    for z in range(NZ):
        for x in range(NX):
            for y in range(NY):
                for c in range(2):
                    tz, tx, ty, tc = move(z, x, y, c)
                    source = (z * NX + x) * NY * 2 + y * 2 + c
                    target = ((tz % NZ) * NX + tx % NX) * NY * 2 + (ty % NY) * 2 + tc
                    pairs.append((source, target))
    return lax.ppermute(array, ("dp", "group"), pairs)


def swap(array):
    return hop(array, lambda z, x, y, c: (z, x, y, 1 - c))


def nt_dot(left, right):
    return lax.dot_general(left, right, (((1,), (1,)), ((), ())), preferred_element_type=F32)


def nn_dot(left, right):
    return lax.dot_general(left, right, (((1,), (0,)), ((), ())), preferred_element_type=F32)


def params(mib):
    return pltpu.CompilerParams(vmem_limit_bytes=mib * MIB)


def whole(array):
    return pl.BlockSpec(array.shape, lambda *_: (0,) * array.ndim)


def like(array):
    return jax.ShapeDtypeStruct(array.shape, array.dtype)


def turn(place, gradient, out):
    for q in range(NY):
        quarter = lax.select(place[2] == 0, lax.rem(place[1] + q, NY), q)
        out[q * 128 : (q + 1) * 128, :] = gradient[pl.ds(pl.multiple_of(quarter * 128, 128), 128), :]


def step_loads(place, source, held, sems):
    i = pl.program_id(0)
    span = NX * 256

    def load(k):
        cols = pl.ds(pl.multiple_of((place[2] * HALF_Z + k) * span, span), span)
        return pltpu.make_async_copy(source.at[:, cols], held.at[k], sems.at[k])

    @pl.when(i == 0)
    def _():
        load(0).start()
        load(1).start()

    @pl.when((i > 0) & (i < HALF_Z - 1))
    def _():
        load(i + 1).start()

    load(i).wait()


def own_kernel(place, number, gradient, source, grads, added, grads_out, turned, held, sems):
    i = pl.program_id(0)

    @pl.when(i == 0)
    def _():
        turn(place, gradient, turned)

    step_loads(place, source, held, sems)
    for at in range(NX):
        added[i, at] = number[0:1, :] * nn_dot(turned[...], held[i, :, at * 256 : (at + 1) * 256])


def other_kernel(place, number, gradient, source, added, s0, plus, minus, s1, s3, turned, held, sems):
    x, c = place[0], place[2]
    i = pl.program_id(0)

    @pl.when(i == 0)
    def _():
        turn(place, gradient, turned)

    step_loads(place, source, held, sems)

    def store(r, j, tile):
        if r == 0:
            s0[j, i] = tile
            return

        @pl.when(j < 2)
        def _():
            if r == 1:
                s1[j, i] = tile
            elif r == 2:
                plus[j, i] = tile
            else:
                minus[2 + j, i] = tile

        @pl.when(j >= 2)
        def _():
            if r == 1:
                plus[j, i] = tile
            elif r == 2:
                minus[j - 2, i] = tile
            else:
                s3[j - 2, i] = tile

    def product(at):
        cols = pl.ds(pl.multiple_of(at * 256, 256), 256)
        return (added[i, at] + number[0:1, :] * nn_dot(turned[...], held[i, :, cols])).astype(BF16)

    @pl.when(c == 0)
    def _():
        for at in range(NX):
            tile = product(at)
            for q in range(NY):
                store(q, at, tile[q * 128 : (q + 1) * 128])

    @pl.when(c == 1)
    def _():
        for r in range(NX):
            tile = product(lax.rem(x + r, NX))
            for q in range(NY):
                store(r, q, tile[q * 128 : (q + 1) * 128])


def partials_scratch(tokens):
    return [
        pltpu.VMEM((512, tokens), BF16),
        pltpu.VMEM((HALF_Z, tokens, NX * 256), BF16),
        pltpu.SemaphoreType.DMA((HALF_Z,)),
    ]


def own_partials(place, number, gradient, inputs, grads):
    tokens = gradient.shape[1]
    shape = jax.ShapeDtypeStruct((HALF_Z, NX, 512, 256), F32)
    vmem = pl.BlockSpec(memory_space=pltpu.VMEM)
    return pl.pallas_call(
        own_kernel,
        grid=(HALF_Z,),
        in_specs=[SMEM, vmem, vmem, HBM, ANYWHERE],
        out_specs=[vmem, ANYWHERE],
        out_shape=[shape, like(grads)],
        scratch_shapes=partials_scratch(tokens),
        input_output_aliases={4: 1},
        compiler_params=params(16),
        cost_estimate=pl.CostEstimate(flops=512 * 512 * 4096, bytes_accessed=4 << 20, transcendentals=0),
    )(place, number, gradient, inputs, grads)


def partials(place, number, gradient, inputs, added):
    tokens = gradient.shape[1]
    jobs = (4, 4, 4, 2, 2)
    vmem = pl.BlockSpec(memory_space=pltpu.VMEM)
    return pl.pallas_call(
        other_kernel,
        grid=(HALF_Z,),
        in_specs=[SMEM, vmem, vmem, HBM, vmem],
        out_specs=[vmem] * 5,
        out_shape=[jax.ShapeDtypeStruct((j, HALF_Z, 128, 256), BF16) for j in jobs],
        scratch_shapes=partials_scratch(tokens),
        compiler_params=params(16),
        cost_estimate=pl.CostEstimate(flops=512 * 512 * 4096, bytes_accessed=8 << 20, transcendentals=0),
    )(place, number, gradient, inputs, added)


def relay_kernel(s1, s3, from_minus, from_plus, *rest):
    s1_out, s3_out = rest[len(rest) // 2 - 1 : len(rest) // 2 + 1]
    s1_out[...] = (s1[...].astype(F32) + from_minus[...].astype(F32)).astype(BF16)
    s3_out[...] = (s3[...].astype(F32) + from_plus[...].astype(F32)).astype(BF16)


def relay(s1, s3, from_minus, from_plus, *through):
    low = pl.BlockSpec((2, 1, 128, 256), lambda i: (0, i, 0, 0))
    count = len(through)
    return pl.pallas_call(
        relay_kernel,
        grid=(HALF_Z,),
        in_specs=[low] * 4 + [ANYWHERE] * count,
        out_specs=[low] * 2 + [ANYWHERE] * count,
        out_shape=[like(a) for a in (s1, s3, *through)],
        input_output_aliases={0: 0, 1: 1} | {4 + k: 2 + k for k in range(count)},
        compiler_params=params(8),
        cost_estimate=pl.CostEstimate(flops=1 << 20, bytes_accessed=3 << 20, transcendentals=0),
    )(s1, s3, from_minus, from_plus, *through)


def first_sum_kernel(place, s0, from_minus, from_plus, late_minus, late_plus, *rest):
    count = (len(rest) - 5) // 2
    added = rest[-1]
    for k in range(2):
        added[k] = s0[k, 0].astype(F32) + (late_minus[k, 0].astype(F32) + from_plus[k, 0].astype(F32))
        added[2 + k] = s0[2 + k, 0].astype(F32) + (late_plus[k, 0].astype(F32) + from_minus[k, 0].astype(F32))
    own = lax.select(place[2] == 0, place[0], place[1])
    for r, u in enumerate(rest[count : count + 4]):
        u[0] = added[lax.rem(own + r, 4)].astype(u.dtype)


def first_sum(place, parts, *through):
    four = pl.BlockSpec((4, 1, 128, 256), lambda i, p: (0, i, 0, 0))
    low = pl.BlockSpec((2, 1, 128, 256), lambda i, p: (0, i, 0, 0))
    high = pl.BlockSpec((2, 1, 128, 256), lambda i, p: (1, i, 0, 0))
    out = pl.BlockSpec((1, 128, 256), lambda i, p: (i, 0, 0))
    shape = (HALF_Z, 128, 256)
    count = len(through)
    return pl.pallas_call(
        first_sum_kernel,
        grid_spec=pltpu.PrefetchScalarGridSpec(
            num_scalar_prefetch=1,
            grid=(HALF_Z,),
            in_specs=[four, high, high, low, low] + [ANYWHERE] * count,
            out_specs=[out] * 4 + [ANYWHERE] * count,
            scratch_shapes=[pltpu.VMEM((4, 128, 256), F32)],
        ),
        out_shape=[jax.ShapeDtypeStruct(shape, F32)]
        + [jax.ShapeDtypeStruct(shape, BF16)] * 3
        + [like(a) for a in through],
        input_output_aliases={6 + k: 4 + k for k in range(count)},
        compiler_params=params(8),
        cost_estimate=pl.CostEstimate(flops=1 << 20, bytes_accessed=4 << 20, transcendentals=0),
    )(place, *parts, *through)


def second_sum_kernel(place, total, a, b, c, d, dep, *rest):
    count = (len(rest) - 4) // 2
    high = jnp.floor(total[...] * (1 / 256))
    ends = jnp.concatenate([high, total[...] - 256 * high], axis=0).astype(BF16)
    for k, v in enumerate(rest[count : count + 4]):
        j = lax.rem(place[3] + k, HALF_Z)
        added = (a[j] + b[j].astype(F32)) + (c[j].astype(F32) + d[j].astype(F32))
        v[0:128, :] = added.astype(v.dtype)
        v[128:144, :] = ends


def second_sum(place, total, parts, dep, *through):
    count = len(through)
    shape = jax.ShapeDtypeStruct((144, 256), BF16)
    return pl.pallas_call(
        second_sum_kernel,
        grid=(1,),
        in_specs=[SMEM, whole(total)] + [whole(a) for a in parts] + [ANYWHERE] * (1 + count),
        out_specs=[whole(shape)] * 4 + [ANYWHERE] * count,
        out_shape=[shape] * 4 + [like(a) for a in through],
        input_output_aliases={7 + k: 4 + k for k in range(count)},
        compiler_params=params(8),
        cost_estimate=pl.CostEstimate(flops=1 << 19, bytes_accessed=1 << 20, transcendentals=0),
    )(place, total, *parts, dep, *through)


def third_sum_kernel(a, b, c, d, *rest):
    out = rest[len(rest) // 2]
    added = (a[...].astype(F32) + b[...].astype(F32)) + (c[...].astype(F32) + d[...].astype(F32))
    out[0:128, :] = added[0:128]
    out[128:136, :] = 256 * added[128:136] + added[136:144]


def third_sum(parts, *through):
    count = len(through)
    shape = jax.ShapeDtypeStruct((136, 256), F32)
    return pl.pallas_call(
        third_sum_kernel,
        grid=(1,),
        in_specs=[whole(a) for a in parts] + [ANYWHERE] * count,
        out_specs=[whole(shape)] + [ANYWHERE] * count,
        out_shape=[shape] + [like(a) for a in through],
        input_output_aliases={4 + k: 1 + k for k in range(count)},
        compiler_params=params(8),
        cost_estimate=pl.CostEstimate(flops=1 << 17, bytes_accessed=1 << 19, transcendentals=0),
    )(*parts, *through)


def merge_kernel(place, own, other, out, half):
    out[...] = own[...] + other[...]
    rows = pl.ds(pl.multiple_of(place[2] * 64, 64), 64)
    half[...] = own[rows, :] + other[rows, :]


def merge(place, own, other):
    half = jax.ShapeDtypeStruct((64, 256), F32)
    vmem = pl.BlockSpec(memory_space=pltpu.VMEM)
    return pl.pallas_call(
        merge_kernel,
        in_specs=[SMEM] + [vmem] * 2,
        out_specs=[vmem] * 2,
        out_shape=[like(own), half],
        compiler_params=params(8),
        cost_estimate=pl.CostEstimate(flops=1 << 16, bytes_accessed=1 << 19, transcendentals=0),
    )(place, own, other)


def after_kernel(*refs):
    pass


def after(*arrays):
    return pl.pallas_call(
        after_kernel,
        in_specs=[ANYWHERE] * len(arrays),
        out_specs=[ANYWHERE] * len(arrays),
        out_shape=[like(a) for a in arrays],
        input_output_aliases={k: k for k in range(len(arrays))},
        compiler_params=params(8),
        cost_estimate=pl.CostEstimate(flops=0, bytes_accessed=0, transcendentals=0),
    )(*arrays)


def assemble_kernel(place, own, near, near_other, far, *rest):
    x, c = place[0], place[2]
    step = 1 - 2 * c
    out = rest[-1]
    rows = own.shape[0]
    to = (x, lax.rem(x - step + NX, NX), lax.rem(x + step + NX, NX), lax.rem(x + 2, NX))
    for at, part in zip(to, (own, near, near_other, far)):
        out[pl.ds(pl.multiple_of(at * rows, rows), rows), :] = part[...]
    out[NX * rows :, :] = jnp.zeros((PAD, out.shape[1]), BF16)


def assemble(place, parts, dep):
    rows, width = parts[0].shape
    shape = jax.ShapeDtypeStruct((NX * rows + PAD, width), BF16)
    return pl.pallas_call(
        assemble_kernel,
        grid=(1,),
        in_specs=[SMEM] + [whole(a) for a in parts] + [ANYWHERE],
        out_specs=whole(shape),
        out_shape=shape,
        compiler_params=params(8),
        cost_estimate=pl.CostEstimate(flops=0, bytes_accessed=2 << 20, transcendentals=0),
    )(place, *parts, dep)


SPAN = 512


def where_to(place, distance, half):
    block = lax.rem(place[3] + distance * (1 - 2 * place[2]) + NZ, NZ)
    return pl.multiple_of((2 * block + half) * SPAN, SPAN)


def products_kernel(grads, *refs):
    chunks, out = refs[:-1], refs[-1]
    for k, chunk in enumerate(chunks):
        for n in range(2):
            out[2 * k + n] = nt_dot(grads[...], chunk[n * SPAN : (n + 1) * SPAN, :])


def products(grads, chunks):
    tokens, width = grads.shape
    pieces = 2 * len(chunks)
    vmem = pl.BlockSpec(memory_space=pltpu.VMEM)
    return pl.pallas_call(
        products_kernel,
        in_specs=[vmem] * (1 + len(chunks)),
        out_specs=vmem,
        out_shape=jax.ShapeDtypeStruct((pieces, tokens, SPAN), F32),
        compiler_params=params(16),
        cost_estimate=pl.CostEstimate(
            flops=2 * tokens * width * SPAN * pieces, bytes_accessed=pieces << 20, transcendentals=0
        ),
    )(grads, *chunks)


def scale_of(filled, total):
    scale = filled[0:1, :] * (DEVICES / total[128:129, :])
    return jnp.concatenate([scale] * (SPAN // 256), axis=1)


def scaled_kernel(distances, place, filled, total, grads, raw, *refs):
    made, out_sems = refs[-2:]
    chunks, out = refs[:-3], refs[-3]
    count = raw.shape[0]
    scale = scale_of(filled, total)
    stores = []
    for n in range(made.shape[0]):
        if n < count:
            piece = raw[n]
        else:
            k, at = divmod(n - count, 2)
            piece = nt_dot(grads[...], chunks[k][at * SPAN : (at + 1) * SPAN, :])
        made[n] = (piece * scale).astype(BF16)
        to = pl.ds(where_to(place, distances[n // 2], n % 2), SPAN)
        stores.append(pltpu.make_async_copy(made.at[n], out.at[:, to], out_sems.at[n]))
        stores[n].start()
    for store in stores:
        store.wait()


def scaled(place, filled, total, grads, raw, raw_distances, chunks, distances):
    tokens = grads.shape[0]
    count = raw.shape[0] + 2 * len(chunks)
    return pl.pallas_call(
        functools.partial(scaled_kernel, (*raw_distances, *distances)),
        in_specs=[SMEM] + [pl.BlockSpec(memory_space=pltpu.VMEM)] * (4 + len(chunks)),
        out_specs=HBM,
        out_shape=jax.ShapeDtypeStruct((tokens, NZ * NX * 256), BF16),
        scratch_shapes=[
            pltpu.VMEM((count, tokens, SPAN), BF16),
            pltpu.SemaphoreType.DMA((count,)),
        ],
        compiler_params=params(16),
        cost_estimate=pl.CostEstimate(flops=count << 17, bytes_accessed=count * 3 << 18, transcendentals=0),
    )(place, filled, total, grads, raw, *chunks)


def finish_kernel(place, filled, own, near, near_other, far, far_other, grads, last, last_other, *rest):
    weight_out, out, made, done, sems = rest[1:]
    y, c = place[1], place[2]
    step = 1 - 2 * c
    scale = scale_of(filled, own)
    stores = []
    for n, chunk in enumerate((last, last_other)):
        made[n] = (nt_dot(grads[...], chunk[...]) * scale).astype(BF16)
        to = pl.ds(where_to(place, HALF_Z, lax.rem(n + c, 2)), SPAN)
        stores.append(pltpu.make_async_copy(made.at[n], out.at[:, to], sems.at[n]))
        stores[n].start()

    inverse = DEVICES / own[128:129, :]

    def put(feature, part):
        done[:, pl.ds(pl.multiple_of(feature * 128, 128), 128)] = (part * inverse).T

    put(y, own[0:128, :])
    put(lax.rem(y - step + NY, NY), near[0:128, :])
    put(lax.rem(y + step + NY, NY), near_other[0:128, :])
    first = jnp.where(c == 0, far[...], far_other[...])
    second = jnp.where(c == 0, far_other[...], far[...])
    put(lax.rem(y + 2, NY), jnp.concatenate([first, second], axis=0))
    stores.append(pltpu.make_async_copy(done, weight_out, sems.at[2]))
    stores[2].start()
    for store in stores:
        store.wait()


def finish(place, filled, parts, grads, lasts, out):
    shape = jax.ShapeDtypeStruct((256, 512), F32)
    tokens = grads.shape[0]
    operands = [place, filled, *parts, grads, *lasts, out]
    return pl.pallas_call(
        finish_kernel,
        in_specs=[SMEM] + [pl.BlockSpec(memory_space=pltpu.VMEM)] * (len(operands) - 2) + [HBM],
        out_specs=[HBM] * 2,
        out_shape=[shape, like(out)],
        scratch_shapes=[
            pltpu.VMEM((2, tokens, SPAN), BF16),
            pltpu.VMEM(shape.shape, F32),
            pltpu.SemaphoreType.DMA((3,)),
        ],
        input_output_aliases={len(operands) - 1: 1},
        compiler_params=params(8),
        cost_estimate=pl.CostEstimate(flops=1 << 28, bytes_accessed=3 << 20, transcendentals=0),
    )(*operands)


def local(inputs, grad_values, value_weight, counts, loss_mask):
    tok_rows = inputs.shape[0]
    dp, group = lax.axis_index("dp"), lax.axis_index("group")
    z, x, y, c = dp // NX, dp % NX, group // 2, group % 2
    place = jnp.stack([x, y, c, z]).astype(jnp.int32)

    other_x = swap(inputs)
    near = hop(value_weight, lambda z, x, y, c: (z, x + 1 - 2 * c, y, c))
    filled = jnp.full((8, 256), counts[0].astype(F32))
    other_filled = swap(filled)
    positions = jnp.arange(tok_rows, dtype=jnp.int32)
    live = (positions < counts[0]) & (loss_mask > 0)
    grads = jnp.where(live[:, None], grad_values, jnp.zeros_like(grad_values))
    own_t = grads.T
    other_t = swap(own_t)

    rows, width = value_weight.shape
    near_other = swap(near)
    far = hop(near, lambda z, x, y, c: (z, x + 1 - 2 * c, y, c))

    added, grads = own_partials(place, filled, own_t, inputs, grads)
    s0, plus, minus, s1, s3 = partials(place, other_filled, other_t, other_x, added)
    s_moves = lambda r: lambda z, x, y, c: (z, x, y + r, c) if c == 0 else (z, x + r, y, c)
    u_moves = lambda r: lambda z, x, y, c: (z, x + r, y, c) if c == 0 else (z, x, y + r, c)
    around = lambda z, x, y, c: (z + 1 - 2 * c, x, y, c)
    chunk = assemble(place, (value_weight, near, near_other, far), s0)

    ring1 = hop(chunk, around)
    from_minus, from_plus = hop(plus, s_moves(1)), hop(minus, s_moves(-1))
    total = filled + other_filled
    total = total + hop(total, lambda z, x, y, c: (z, x, y + 1, c))
    s1, s3, ring1, total = relay(s1, s3, from_minus, from_plus, ring1, total)

    ring2, ring1_other = hop(ring1, around), swap(ring1)
    first = (s0, from_minus, from_plus, hop(s1, s_moves(1)), hop(s3, s_moves(-1)))
    total = total + hop(total, lambda z, x, y, c: (z, x + 1, y, c))
    total = total + hop(total, lambda z, x, y, c: (z, x, y + 2, c))
    u0, u1, u2, u3, ring2, ring1_other, total = first_sum(place, first, ring2, ring1_other, total)

    ring3, ring2_other = hop(ring2, around), swap(ring2)
    second = [u0] + [hop(u, u_moves(r)) for r, u in ((1, u1), (2, u2), (3, u3))]
    total = total + hop(total, lambda z, x, y, c: (z, x + 2, y, c))
    raw = products(grads, (chunk, ring1, ring1_other, ring2, ring2_other))
    *sends, ring3 = second_sum(place, total, second, raw, ring3)

    half = NX * rows // 2
    last = lax.dynamic_slice(ring3, (c * half, 0), (half, width))
    ring3_other = swap(ring3)
    third = [
        hop(sends[k], lambda z, x, y, c: (HALF_Z * c + (z + k) % HALF_Z, x, y, z // HALF_Z)) for k in range(4)
    ]
    block, last, ring3, ring3_other = third_sum(third, last, ring3, ring3_other)

    last = hop(last, around)
    block, part = merge(place, block, swap(block))
    near = hop(block, lambda z, x, y, c: (z, x, y + 1 - 2 * c, c))
    far = hop(part, lambda z, x, y, c: (z, x, y + 2, c))
    input_grad = scaled(place, filled, block, grads, raw, (0, -1, 1, -2, 2), (ring3, ring3_other), (-3, 3))
    near, far, last, input_grad = after(near, far, last, input_grad)
    parts = (block, near, swap(near), far, swap(far))
    weight_grad, input_grad = finish(place, filled, parts, grads, (last, swap(last)), input_grad)
    return (input_grad, weight_grad)


def solution(mesh):
    return jax.shard_map(
        local,
        mesh=mesh,
        in_specs=(
            P(("dp", "group"), None),
            P(("dp", "group"), None),
            P("dp", None),
            P(("dp", "group")),
            P(("dp", "group")),
        ),
        out_specs=(P(("dp", "group"), None), P("dp", None)),
        check_vma=False,
    )
```

```python
import functools

import jax
import jax.numpy as jnp
from jax import lax
from jax.experimental import pallas as pl
from jax.experimental.pallas import tpu as pltpu
from jax.sharding import PartitionSpec as P

NZ, NX, NY = 8, 4, 4
HALF_Z = NZ // 2
DEVICES = NZ * NX * NY * 2
PAD = 16
F32, BF16 = jnp.float32, jnp.bfloat16
MIB = 1 << 20
ANYWHERE = pl.BlockSpec(memory_space=pl.ANY)
HBM = pl.BlockSpec(memory_space=pltpu.HBM)
SMEM = pl.BlockSpec(memory_space=pltpu.SMEM)


def hop(array, move):
    pairs = []
    for z in range(NZ):
        for x in range(NX):
            for y in range(NY):
                for c in range(2):
                    tz, tx, ty, tc = move(z, x, y, c)
                    source = (z * NX + x) * NY * 2 + y * 2 + c
                    target = ((tz % NZ) * NX + tx % NX) * NY * 2 + (ty % NY) * 2 + tc
                    pairs.append((source, target))
    return lax.ppermute(array, ("dp", "group"), pairs)


def swap(array):
    return hop(array, lambda z, x, y, c: (z, x, y, 1 - c))


def nt_dot(left, right):
    return lax.dot_general(left, right, (((1,), (1,)), ((), ())), preferred_element_type=F32)


def nn_dot(left, right):
    return lax.dot_general(left, right, (((1,), (0,)), ((), ())), preferred_element_type=F32)


def params(mib):
    return pltpu.CompilerParams(vmem_limit_bytes=mib * MIB)


def whole(array):
    return pl.BlockSpec(array.shape, lambda *_: (0,) * array.ndim)


def like(array):
    return jax.ShapeDtypeStruct(array.shape, array.dtype)


def turn(place, gradient, out):
    for q in range(NY):
        quarter = lax.select(place[2] == 0, lax.rem(place[1] + q, NY), q)
        out[q * 128 : (q + 1) * 128, :] = gradient[pl.ds(pl.multiple_of(quarter * 128, 128), 128), :]


def step_loads(place, source, held, sems):
    i = pl.program_id(0)
    span = NX * 256

    def load(k):
        far = lax.select(place[2] == 0, jnp.int32(k), jnp.where(k == 0, HALF_Z, NZ - k).astype(jnp.int32))
        cols = pl.ds(pl.multiple_of(lax.rem(place[3] + far, NZ) * span, span), span)
        return pltpu.make_async_copy(source.at[:, cols], held.at[k], sems.at[k])

    @pl.when(i == 0)
    def _():
        load(0).start()
        load(1).start()

    @pl.when((i > 0) & (i < HALF_Z - 1))
    def _():
        load(i + 1).start()

    load(i).wait()


def own_kernel(place, number, gradient, source, grads, added, grads_out, turned, held, sems):
    i = pl.program_id(0)

    @pl.when(i == 0)
    def _():
        turn(place, gradient, turned)

    step_loads(place, source, held, sems)
    for at in range(NX):
        added[i, at] = number[0:1, :] * nn_dot(turned[...], held[i, :, at * 256 : (at + 1) * 256])


def other_kernel(place, number, gradient, source, added, s0, plus, minus, s1, s3, turned, held, sems):
    x, c = place[0], place[2]
    i = pl.program_id(0)

    @pl.when(i == 0)
    def _():
        turn(place, gradient, turned)

    step_loads(place, source, held, sems)

    def store(r, j, tile):
        if r == 0:
            s0[j, i] = tile
            return

        @pl.when(j < 2)
        def _():
            if r == 1:
                s1[j, i] = tile
            elif r == 2:
                plus[j, i] = tile
            else:
                minus[2 + j, i] = tile

        @pl.when(j >= 2)
        def _():
            if r == 1:
                plus[j, i] = tile
            elif r == 2:
                minus[j - 2, i] = tile
            else:
                s3[j - 2, i] = tile

    def product(at):
        cols = pl.ds(pl.multiple_of(at * 256, 256), 256)
        return (added[i, at] + number[0:1, :] * nn_dot(turned[...], held[i, :, cols])).astype(BF16)

    @pl.when(c == 0)
    def _():
        for at in range(NX):
            tile = product(at)
            for q in range(NY):
                store(q, at, tile[q * 128 : (q + 1) * 128])

    @pl.when(c == 1)
    def _():
        for r in range(NX):
            tile = product(lax.rem(x + r, NX))
            for q in range(NY):
                store(r, q, tile[q * 128 : (q + 1) * 128])


def partials_scratch(tokens):
    return [
        pltpu.VMEM((512, tokens), BF16),
        pltpu.VMEM((HALF_Z, tokens, NX * 256), BF16),
        pltpu.SemaphoreType.DMA((HALF_Z,)),
    ]


def own_partials(place, number, gradient, inputs, grads):
    tokens = gradient.shape[1]
    shape = jax.ShapeDtypeStruct((HALF_Z, NX, 512, 256), F32)
    vmem = pl.BlockSpec(memory_space=pltpu.VMEM)
    return pl.pallas_call(
        own_kernel,
        grid=(HALF_Z,),
        in_specs=[SMEM, vmem, vmem, HBM, ANYWHERE],
        out_specs=[vmem, ANYWHERE],
        out_shape=[shape, like(grads)],
        scratch_shapes=partials_scratch(tokens),
        input_output_aliases={4: 1},
        compiler_params=params(16),
        cost_estimate=pl.CostEstimate(flops=512 * 512 * 4096, bytes_accessed=4 << 20, transcendentals=0),
    )(place, number, gradient, inputs, grads)


def partials(place, number, gradient, inputs, added):
    tokens = gradient.shape[1]
    jobs = (4, 4, 4, 2, 2)
    vmem = pl.BlockSpec(memory_space=pltpu.VMEM)
    return pl.pallas_call(
        other_kernel,
        grid=(HALF_Z,),
        in_specs=[SMEM, vmem, vmem, HBM, vmem],
        out_specs=[vmem] * 5,
        out_shape=[jax.ShapeDtypeStruct((j, HALF_Z, 128, 256), BF16) for j in jobs],
        scratch_shapes=partials_scratch(tokens),
        compiler_params=params(16),
        cost_estimate=pl.CostEstimate(flops=512 * 512 * 4096, bytes_accessed=8 << 20, transcendentals=0),
    )(place, number, gradient, inputs, added)


def relay_kernel(s1, s3, from_minus, from_plus, *rest):
    s1_out, s3_out = rest[len(rest) // 2 - 1 : len(rest) // 2 + 1]
    s1_out[...] = (s1[...].astype(F32) + from_minus[...].astype(F32)).astype(BF16)
    s3_out[...] = (s3[...].astype(F32) + from_plus[...].astype(F32)).astype(BF16)


def relay(s1, s3, from_minus, from_plus, *through):
    low = pl.BlockSpec((2, 1, 128, 256), lambda i: (0, i, 0, 0))
    count = len(through)
    return pl.pallas_call(
        relay_kernel,
        grid=(HALF_Z,),
        in_specs=[low] * 4 + [ANYWHERE] * count,
        out_specs=[low] * 2 + [ANYWHERE] * count,
        out_shape=[like(a) for a in (s1, s3, *through)],
        input_output_aliases={0: 0, 1: 1} | {4 + k: 2 + k for k in range(count)},
        compiler_params=params(8),
        cost_estimate=pl.CostEstimate(flops=1 << 20, bytes_accessed=3 << 20, transcendentals=0),
    )(s1, s3, from_minus, from_plus, *through)


def first_sum_kernel(place, s0, from_minus, from_plus, late_minus, late_plus, *rest):
    count = (len(rest) - 5) // 2
    added = rest[-1]
    for k in range(2):
        added[k] = s0[k, 0].astype(F32) + (late_minus[k, 0].astype(F32) + from_plus[k, 0].astype(F32))
        added[2 + k] = s0[2 + k, 0].astype(F32) + (late_plus[k, 0].astype(F32) + from_minus[k, 0].astype(F32))
    own = lax.select(place[2] == 0, place[0], place[1])
    for r, u in enumerate(rest[count : count + 4]):
        u[0] = added[lax.rem(own + r, 4)].astype(u.dtype)


def first_sum(place, parts, *through):
    four = pl.BlockSpec((4, 1, 128, 256), lambda i, p: (0, i, 0, 0))
    low = pl.BlockSpec((2, 1, 128, 256), lambda i, p: (0, i, 0, 0))
    high = pl.BlockSpec((2, 1, 128, 256), lambda i, p: (1, i, 0, 0))
    out = pl.BlockSpec((1, 128, 256), lambda i, p: (i, 0, 0))
    shape = (HALF_Z, 128, 256)
    count = len(through)
    return pl.pallas_call(
        first_sum_kernel,
        grid_spec=pltpu.PrefetchScalarGridSpec(
            num_scalar_prefetch=1,
            grid=(HALF_Z,),
            in_specs=[four, high, high, low, low] + [ANYWHERE] * count,
            out_specs=[out] * 4 + [ANYWHERE] * count,
            scratch_shapes=[pltpu.VMEM((4, 128, 256), F32)],
        ),
        out_shape=[jax.ShapeDtypeStruct(shape, F32)]
        + [jax.ShapeDtypeStruct(shape, BF16)] * 3
        + [like(a) for a in through],
        input_output_aliases={6 + k: 4 + k for k in range(count)},
        compiler_params=params(8),
        cost_estimate=pl.CostEstimate(flops=1 << 20, bytes_accessed=4 << 20, transcendentals=0),
    )(place, *parts, *through)


def second_sum_kernel(place, total, a, b, c, d, dep, *rest):
    count = (len(rest) - 4) // 2
    high = jnp.floor(total[...] * (1 / 256))
    ends = jnp.concatenate([high, total[...] - 256 * high], axis=0).astype(BF16)
    for k, v in enumerate(rest[count : count + 4]):
        added = (a[k] + b[k].astype(F32)) + (c[k].astype(F32) + d[k].astype(F32))
        v[0:128, :] = added.astype(v.dtype)
        v[128:144, :] = ends


def second_sum(place, total, parts, dep, *through):
    count = len(through)
    shape = jax.ShapeDtypeStruct((144, 256), BF16)
    return pl.pallas_call(
        second_sum_kernel,
        grid=(1,),
        in_specs=[SMEM, whole(total)] + [whole(a) for a in parts] + [ANYWHERE] * (1 + count),
        out_specs=[whole(shape)] * 4 + [ANYWHERE] * count,
        out_shape=[shape] * 4 + [like(a) for a in through],
        input_output_aliases={7 + k: 4 + k for k in range(count)},
        compiler_params=params(8),
        cost_estimate=pl.CostEstimate(flops=1 << 19, bytes_accessed=1 << 20, transcendentals=0),
    )(place, total, *parts, dep, *through)


def third_sum_kernel(a, b, c, d, *rest):
    out = rest[len(rest) // 2]
    added = (a[...].astype(F32) + b[...].astype(F32)) + (c[...].astype(F32) + d[...].astype(F32))
    out[0:128, :] = added[0:128]
    out[128:136, :] = 256 * added[128:136] + added[136:144]


def third_sum(parts, *through):
    count = len(through)
    shape = jax.ShapeDtypeStruct((136, 256), F32)
    return pl.pallas_call(
        third_sum_kernel,
        grid=(1,),
        in_specs=[whole(a) for a in parts] + [ANYWHERE] * count,
        out_specs=[whole(shape)] + [ANYWHERE] * count,
        out_shape=[shape] + [like(a) for a in through],
        input_output_aliases={4 + k: 1 + k for k in range(count)},
        compiler_params=params(8),
        cost_estimate=pl.CostEstimate(flops=1 << 17, bytes_accessed=1 << 19, transcendentals=0),
    )(*parts, *through)


def merge_kernel(place, own, other, out, half):
    out[...] = own[...] + other[...]
    rows = pl.ds(pl.multiple_of(place[2] * 64, 64), 64)
    half[...] = own[rows, :] + other[rows, :]


def merge(place, own, other):
    half = jax.ShapeDtypeStruct((64, 256), F32)
    vmem = pl.BlockSpec(memory_space=pltpu.VMEM)
    return pl.pallas_call(
        merge_kernel,
        in_specs=[SMEM] + [vmem] * 2,
        out_specs=[vmem] * 2,
        out_shape=[like(own), half],
        compiler_params=params(8),
        cost_estimate=pl.CostEstimate(flops=1 << 16, bytes_accessed=1 << 19, transcendentals=0),
    )(place, own, other)


def after_kernel(*refs):
    pass


def after(*arrays):
    return pl.pallas_call(
        after_kernel,
        in_specs=[ANYWHERE] * len(arrays),
        out_specs=[ANYWHERE] * len(arrays),
        out_shape=[like(a) for a in arrays],
        input_output_aliases={k: k for k in range(len(arrays))},
        compiler_params=params(8),
        cost_estimate=pl.CostEstimate(flops=0, bytes_accessed=0, transcendentals=0),
    )(*arrays)


def assemble_kernel(place, own, near, near_other, far, *rest):
    x, c = place[0], place[2]
    step = 1 - 2 * c
    out = rest[-1]
    rows = own.shape[0]
    to = (x, lax.rem(x - step + NX, NX), lax.rem(x + step + NX, NX), lax.rem(x + 2, NX))
    for at, part in zip(to, (own, near, near_other, far)):
        out[pl.ds(pl.multiple_of(at * rows, rows), rows), :] = part[...]
    out[NX * rows :, :] = jnp.zeros((PAD, out.shape[1]), BF16)


def assemble(place, parts, dep):
    rows, width = parts[0].shape
    shape = jax.ShapeDtypeStruct((NX * rows + PAD, width), BF16)
    return pl.pallas_call(
        assemble_kernel,
        grid=(1,),
        in_specs=[SMEM] + [whole(a) for a in parts] + [ANYWHERE],
        out_specs=whole(shape),
        out_shape=shape,
        compiler_params=params(8),
        cost_estimate=pl.CostEstimate(flops=0, bytes_accessed=2 << 20, transcendentals=0),
    )(place, *parts, dep)


SPAN = 512


def where_to(place, distance, half):
    block = lax.rem(place[3] + distance * (1 - 2 * place[2]) + NZ, NZ)
    return pl.multiple_of((2 * block + half) * SPAN, SPAN)


def products_kernel(grads, *refs):
    chunks, out = refs[:-1], refs[-1]
    for k, chunk in enumerate(chunks):
        for n in range(2):
            out[2 * k + n] = nt_dot(grads[...], chunk[n * SPAN : (n + 1) * SPAN, :])


def products(grads, chunks):
    tokens, width = grads.shape
    pieces = 2 * len(chunks)
    vmem = pl.BlockSpec(memory_space=pltpu.VMEM)
    return pl.pallas_call(
        products_kernel,
        in_specs=[vmem] * (1 + len(chunks)),
        out_specs=vmem,
        out_shape=jax.ShapeDtypeStruct((pieces, tokens, SPAN), F32),
        compiler_params=params(16),
        cost_estimate=pl.CostEstimate(
            flops=2 * tokens * width * SPAN * pieces, bytes_accessed=pieces << 20, transcendentals=0
        ),
    )(grads, *chunks)


def scale_of(filled, total):
    scale = filled[0:1, :] * (DEVICES / total[128:129, :])
    return jnp.concatenate([scale] * (SPAN // 256), axis=1)


def scaled_kernel(distances, place, filled, total, grads, raw, *refs):
    made, out_sems = refs[-2:]
    chunks, out = refs[:-3], refs[-3]
    count = raw.shape[0]
    scale = scale_of(filled, total)
    stores = []
    for n in range(made.shape[0]):
        if n < count:
            piece = raw[n]
        else:
            k, at = divmod(n - count, 2)
            piece = nt_dot(grads[...], chunks[k][at * SPAN : (at + 1) * SPAN, :])
        made[n] = (piece * scale).astype(BF16)
        to = pl.ds(where_to(place, distances[n // 2], n % 2), SPAN)
        stores.append(pltpu.make_async_copy(made.at[n], out.at[:, to], out_sems.at[n]))
        stores[n].start()
    for store in stores:
        store.wait()


def scaled(place, filled, total, grads, raw, raw_distances, chunks, distances):
    tokens = grads.shape[0]
    count = raw.shape[0] + 2 * len(chunks)
    return pl.pallas_call(
        functools.partial(scaled_kernel, (*raw_distances, *distances)),
        in_specs=[SMEM] + [pl.BlockSpec(memory_space=pltpu.VMEM)] * (4 + len(chunks)),
        out_specs=HBM,
        out_shape=jax.ShapeDtypeStruct((tokens, NZ * NX * 256), BF16),
        scratch_shapes=[
            pltpu.VMEM((count, tokens, SPAN), BF16),
            pltpu.SemaphoreType.DMA((count,)),
        ],
        compiler_params=params(16),
        cost_estimate=pl.CostEstimate(flops=count << 17, bytes_accessed=count * 3 << 18, transcendentals=0),
    )(place, filled, total, grads, raw, *chunks)


def finish_kernel(place, filled, own, near, near_other, far, far_other, grads, last, last_other, *rest):
    weight_out, out, made, done, sems = rest[1:]
    y, c = place[1], place[2]
    step = 1 - 2 * c
    scale = scale_of(filled, own)
    stores = []
    for n, chunk in enumerate((last, last_other)):
        made[n] = (nt_dot(grads[...], chunk[...]) * scale).astype(BF16)
        to = pl.ds(where_to(place, HALF_Z, lax.rem(n + c, 2)), SPAN)
        stores.append(pltpu.make_async_copy(made.at[n], out.at[:, to], sems.at[n]))
        stores[n].start()

    inverse = DEVICES / own[128:129, :]

    def put(feature, part):
        done[:, pl.ds(pl.multiple_of(feature * 128, 128), 128)] = (part * inverse).T

    put(y, own[0:128, :])
    put(lax.rem(y - step + NY, NY), near[0:128, :])
    put(lax.rem(y + step + NY, NY), near_other[0:128, :])
    first = jnp.where(c == 0, far[...], far_other[...])
    second = jnp.where(c == 0, far_other[...], far[...])
    put(lax.rem(y + 2, NY), jnp.concatenate([first, second], axis=0))
    stores.append(pltpu.make_async_copy(done, weight_out, sems.at[2]))
    stores[2].start()
    for store in stores:
        store.wait()


def finish(place, filled, parts, grads, lasts, out):
    shape = jax.ShapeDtypeStruct((256, 512), F32)
    tokens = grads.shape[0]
    operands = [place, filled, *parts, grads, *lasts, out]
    return pl.pallas_call(
        finish_kernel,
        in_specs=[SMEM] + [pl.BlockSpec(memory_space=pltpu.VMEM)] * (len(operands) - 2) + [HBM],
        out_specs=[HBM] * 2,
        out_shape=[shape, like(out)],
        scratch_shapes=[
            pltpu.VMEM((2, tokens, SPAN), BF16),
            pltpu.VMEM(shape.shape, F32),
            pltpu.SemaphoreType.DMA((3,)),
        ],
        input_output_aliases={len(operands) - 1: 1},
        compiler_params=params(8),
        cost_estimate=pl.CostEstimate(flops=1 << 28, bytes_accessed=3 << 20, transcendentals=0),
    )(*operands)


def local(inputs, grad_values, value_weight, counts, loss_mask):
    tok_rows = inputs.shape[0]
    dp, group = lax.axis_index("dp"), lax.axis_index("group")
    z, x, y, c = dp // NX, dp % NX, group // 2, group % 2
    place = jnp.stack([x, y, c, z]).astype(jnp.int32)

    other_x = swap(inputs)
    near = hop(value_weight, lambda z, x, y, c: (z, x + 1 - 2 * c, y, c))
    filled = jnp.full((8, 256), counts[0].astype(F32))
    other_filled = swap(filled)
    positions = jnp.arange(tok_rows, dtype=jnp.int32)
    live = (positions < counts[0]) & (loss_mask > 0)
    grads = jnp.where(live[:, None], grad_values, jnp.zeros_like(grad_values))
    own_t = grads.T
    other_t = swap(own_t)

    rows, width = value_weight.shape
    near_other = swap(near)
    far = hop(near, lambda z, x, y, c: (z, x + 1 - 2 * c, y, c))

    added, grads = own_partials(place, filled, own_t, inputs, grads)
    s0, plus, minus, s1, s3 = partials(place, other_filled, other_t, other_x, added)
    s_moves = lambda r: lambda z, x, y, c: (z, x, y + r, c) if c == 0 else (z, x + r, y, c)
    u_moves = lambda r: lambda z, x, y, c: (z, x + r, y, c) if c == 0 else (z, x, y + r, c)
    around = lambda z, x, y, c: (z + 1 - 2 * c, x, y, c)
    chunk = assemble(place, (value_weight, near, near_other, far), s0)

    ring1 = hop(chunk, around)
    from_minus, from_plus = hop(plus, s_moves(1)), hop(minus, s_moves(-1))
    total = filled + other_filled
    total = total + hop(total, lambda z, x, y, c: (z, x, y + 1, c))
    s1, s3, ring1, total = relay(s1, s3, from_minus, from_plus, ring1, total)

    ring2, ring1_other = hop(ring1, around), swap(ring1)
    first = (s0, from_minus, from_plus, hop(s1, s_moves(1)), hop(s3, s_moves(-1)))
    total = total + hop(total, lambda z, x, y, c: (z, x + 1, y, c))
    total = total + hop(total, lambda z, x, y, c: (z, x, y + 2, c))
    u0, u1, u2, u3, ring2, ring1_other, total = first_sum(place, first, ring2, ring1_other, total)

    ring3, ring2_other = hop(ring2, around), swap(ring2)
    second = [u0] + [hop(u, u_moves(r)) for r, u in ((1, u1), (2, u2), (3, u3))]
    total = total + hop(total, lambda z, x, y, c: (z, x + 2, y, c))
    raw = products(grads, (chunk, ring1, ring1_other, ring2, ring2_other))
    *sends, ring3 = second_sum(place, total, second, raw, ring3)

    half = NX * rows // 2
    last = lax.dynamic_slice(ring3, (c * half, 0), (half, width))
    ring3_other = swap(ring3)
    third = [hop(sends[0], lambda z, x, y, c: (z + HALF_Z * c, x, y, c))]
    third += [hop(sends[k], lambda z, x, y, c: (z + k * (1 - 2 * c), x, y, c)) for k in range(1, HALF_Z)]
    block, last, ring3, ring3_other = third_sum(third, last, ring3, ring3_other)

    last = hop(last, around)
    block, part = merge(place, block, swap(block))
    near = hop(block, lambda z, x, y, c: (z, x, y + 1 - 2 * c, c))
    far = hop(part, lambda z, x, y, c: (z, x, y + 2, c))
    input_grad = scaled(place, filled, block, grads, raw, (0, -1, 1, -2, 2), (ring3, ring3_other), (-3, 3))
    near, far, last, input_grad = after(near, far, last, input_grad)
    parts = (block, near, swap(near), far, swap(far))
    weight_grad, input_grad = finish(place, filled, parts, grads, (last, swap(last)), input_grad)
    return (input_grad, weight_grad)


def solution(mesh):
    return jax.shard_map(
        local,
        mesh=mesh,
        in_specs=(
            P(("dp", "group"), None),
            P(("dp", "group"), None),
            P("dp", None),
            P(("dp", "group")),
            P(("dp", "group")),
        ),
        out_specs=(P(("dp", "group"), None), P("dp", None)),
        check_vma=False,
    )
```

```python
import functools

import jax
import jax.numpy as jnp
from jax import lax
from jax.experimental import pallas as pl
from jax.experimental.pallas import tpu as pltpu
from jax.sharding import PartitionSpec as P

NZ, NX, NY = 8, 4, 4
HALF_Z = NZ // 2
DEVICES = NZ * NX * NY * 2
PAD = 16
F32, BF16 = jnp.float32, jnp.bfloat16
MIB = 1 << 20
ANYWHERE = pl.BlockSpec(memory_space=pl.ANY)
HBM = pl.BlockSpec(memory_space=pltpu.HBM)
SMEM = pl.BlockSpec(memory_space=pltpu.SMEM)


def hop(array, move):
    pairs = []
    for z in range(NZ):
        for x in range(NX):
            for y in range(NY):
                for c in range(2):
                    tz, tx, ty, tc = move(z, x, y, c)
                    source = (z * NX + x) * NY * 2 + y * 2 + c
                    target = ((tz % NZ) * NX + tx % NX) * NY * 2 + (ty % NY) * 2 + tc
                    pairs.append((source, target))
    return lax.ppermute(array, ("dp", "group"), pairs)


def swap(array):
    return hop(array, lambda z, x, y, c: (z, x, y, 1 - c))


def nt_dot(left, right):
    return lax.dot_general(left, right, (((1,), (1,)), ((), ())), preferred_element_type=F32)


def nn_dot(left, right):
    return lax.dot_general(left, right, (((1,), (0,)), ((), ())), preferred_element_type=F32)


def params(mib):
    return pltpu.CompilerParams(vmem_limit_bytes=mib * MIB)


def whole(array):
    return pl.BlockSpec(array.shape, lambda *_: (0,) * array.ndim)


def like(array):
    return jax.ShapeDtypeStruct(array.shape, array.dtype)


def turn(place, gradient, out):
    for q in range(NY):
        quarter = lax.select(place[2] == 0, lax.rem(place[1] + q, NY), q)
        out[q * 128 : (q + 1) * 128, :] = gradient[pl.ds(pl.multiple_of(quarter * 128, 128), 128), :]


def step_loads(place, source, held, sems):
    i = pl.program_id(0)
    span = NX * 256

    def load(k):
        far = lax.select(place[2] == 0, jnp.int32(k), jnp.where(k == 0, HALF_Z, NZ - k).astype(jnp.int32))
        cols = pl.ds(pl.multiple_of(lax.rem(place[3] + far, NZ) * span, span), span)
        return pltpu.make_async_copy(source.at[:, cols], held.at[k], sems.at[k])

    @pl.when(i == 0)
    def _():
        load(0).start()
        load(1).start()

    @pl.when((i > 0) & (i < HALF_Z - 1))
    def _():
        load(i + 1).start()

    load(i).wait()


def own_kernel(place, number, gradient, source, grads, added, grads_out, turned, held, sems):
    i = pl.program_id(0)

    @pl.when(i == 0)
    def _():
        turn(place, gradient, turned)

    step_loads(place, source, held, sems)
    for at in range(NX):
        added[i, at] = number[0:1, :] * nn_dot(turned[...], held[i, :, at * 256 : (at + 1) * 256])


def other_kernel(place, number, gradient, source, added, s0, plus, minus, s1, s3, turned, held, sems):
    x, c = place[0], place[2]
    i = pl.program_id(0)

    @pl.when(i == 0)
    def _():
        turn(place, gradient, turned)

    step_loads(place, source, held, sems)

    def store(r, j, tile):
        if r == 0:
            s0[j, i] = tile
            return

        @pl.when(j < 2)
        def _():
            if r == 1:
                s1[j, i] = tile
            elif r == 2:
                plus[j, i] = tile
            else:
                minus[2 + j, i] = tile

        @pl.when(j >= 2)
        def _():
            if r == 1:
                plus[j, i] = tile
            elif r == 2:
                minus[j - 2, i] = tile
            else:
                s3[j - 2, i] = tile

    def product(at):
        cols = pl.ds(pl.multiple_of(at * 256, 256), 256)
        return (added[i, at] + number[0:1, :] * nn_dot(turned[...], held[i, :, cols])).astype(BF16)

    @pl.when(c == 0)
    def _():
        for at in range(NX):
            tile = product(at)
            for q in range(NY):
                store(q, at, tile[q * 128 : (q + 1) * 128])

    @pl.when(c == 1)
    def _():
        for r in range(NX):
            tile = product(lax.rem(x + r, NX))
            for q in range(NY):
                store(r, q, tile[q * 128 : (q + 1) * 128])


def partials_scratch(tokens):
    return [
        pltpu.VMEM((512, tokens), BF16),
        pltpu.VMEM((HALF_Z, tokens, NX * 256), BF16),
        pltpu.SemaphoreType.DMA((HALF_Z,)),
    ]


def own_partials(place, number, gradient, inputs, grads):
    tokens = gradient.shape[1]
    shape = jax.ShapeDtypeStruct((HALF_Z, NX, 512, 256), F32)
    vmem = pl.BlockSpec(memory_space=pltpu.VMEM)
    return pl.pallas_call(
        own_kernel,
        grid=(HALF_Z,),
        in_specs=[SMEM, vmem, vmem, HBM, ANYWHERE],
        out_specs=[vmem, ANYWHERE],
        out_shape=[shape, like(grads)],
        scratch_shapes=partials_scratch(tokens),
        input_output_aliases={4: 1},
        compiler_params=params(16),
        cost_estimate=pl.CostEstimate(flops=512 * 512 * 4096, bytes_accessed=4 << 20, transcendentals=0),
    )(place, number, gradient, inputs, grads)


def partials(place, number, gradient, inputs, added):
    tokens = gradient.shape[1]
    jobs = (4, 4, 4, 2, 2)
    vmem = pl.BlockSpec(memory_space=pltpu.VMEM)
    return pl.pallas_call(
        other_kernel,
        grid=(HALF_Z,),
        in_specs=[SMEM, vmem, vmem, HBM, vmem],
        out_specs=[vmem] * 5,
        out_shape=[jax.ShapeDtypeStruct((j, HALF_Z, 128, 256), BF16) for j in jobs],
        scratch_shapes=partials_scratch(tokens),
        compiler_params=params(16),
        cost_estimate=pl.CostEstimate(flops=512 * 512 * 4096, bytes_accessed=8 << 20, transcendentals=0),
    )(place, number, gradient, inputs, added)


def relay_kernel(s1, s3, from_minus, from_plus, *rest):
    s1_out, s3_out = rest[len(rest) // 2 - 1 : len(rest) // 2 + 1]
    s1_out[...] = (s1[...].astype(F32) + from_minus[...].astype(F32)).astype(BF16)
    s3_out[...] = (s3[...].astype(F32) + from_plus[...].astype(F32)).astype(BF16)


def relay(s1, s3, from_minus, from_plus, *through):
    low = pl.BlockSpec((2, 1, 128, 256), lambda i: (0, i, 0, 0))
    count = len(through)
    return pl.pallas_call(
        relay_kernel,
        grid=(HALF_Z,),
        in_specs=[low] * 4 + [ANYWHERE] * count,
        out_specs=[low] * 2 + [ANYWHERE] * count,
        out_shape=[like(a) for a in (s1, s3, *through)],
        input_output_aliases={0: 0, 1: 1} | {4 + k: 2 + k for k in range(count)},
        compiler_params=params(8),
        cost_estimate=pl.CostEstimate(flops=1 << 20, bytes_accessed=3 << 20, transcendentals=0),
    )(s1, s3, from_minus, from_plus, *through)


def split_count(total):
    high = jnp.floor(total * (1 / 256))
    return jnp.concatenate([high, total - 256 * high], axis=0)


def first_sum_kernel(place, total, s0, from_minus, from_plus, late_minus, late_plus, u0, u1, u2, u3, added):
    i = pl.program_id(0)
    for k in range(2):
        added[k] = s0[k, 0].astype(F32) + (late_minus[k, 0].astype(F32) + from_plus[k, 0].astype(F32))
        added[2 + k] = s0[2 + k, 0].astype(F32) + (late_plus[k, 0].astype(F32) + from_minus[k, 0].astype(F32))
    own = lax.select(place[2] == 0, place[0], place[1])
    rows = pl.ds(pl.multiple_of(i * 128, 128), 128)
    for r, u in enumerate((u0, u1, u2, u3)):
        u[rows, :] = added[lax.rem(own + r, 4)].astype(u.dtype)

    @pl.when(i == 0)
    def _():
        ends = split_count(total[...])
        for u in (u0, u1, u2, u3):
            u[HALF_Z * 128 :, :] = ends.astype(u.dtype)


def first_sum(place, total, parts):
    four = pl.BlockSpec((4, 1, 128, 256), lambda i: (0, i, 0, 0))
    low = pl.BlockSpec((2, 1, 128, 256), lambda i: (0, i, 0, 0))
    high = pl.BlockSpec((2, 1, 128, 256), lambda i: (1, i, 0, 0))
    vmem = pl.BlockSpec(memory_space=pltpu.VMEM)
    shape = (HALF_Z * 128 + 16, 256)
    return pl.pallas_call(
        first_sum_kernel,
        grid=(HALF_Z,),
        in_specs=[SMEM, vmem, four, high, high, low, low],
        out_specs=[vmem] * 4,
        out_shape=[jax.ShapeDtypeStruct(shape, F32)] + [jax.ShapeDtypeStruct(shape, BF16)] * 3,
        scratch_shapes=[pltpu.VMEM((4, 128, 256), F32)],
        compiler_params=params(8),
        cost_estimate=pl.CostEstimate(flops=1 << 20, bytes_accessed=4 << 20, transcendentals=0),
    )(place, total, *parts)


def second_sum_kernel(a, b, c, d, dep, *rest):
    count = (len(rest) - 4) // 2
    ends = HALF_Z * 128

    def added(rows):
        return (a[rows, :] + b[rows, :].astype(F32)) + (c[rows, :].astype(F32) + d[rows, :].astype(F32))

    counts = added(slice(ends, ends + 16))
    counts = split_count(256 * counts[0:8] + counts[8:16])
    for k, v in enumerate(rest[count : count + 4]):
        v[0:128, :] = added(slice(k * 128, (k + 1) * 128)).astype(v.dtype)
        v[128:144, :] = counts.astype(v.dtype)


def second_sum(parts, dep, *through):
    count = len(through)
    shape = jax.ShapeDtypeStruct((144, 256), BF16)
    return pl.pallas_call(
        second_sum_kernel,
        grid=(1,),
        in_specs=[whole(a) for a in parts] + [ANYWHERE] * (1 + count),
        out_specs=[whole(shape)] * 4 + [ANYWHERE] * count,
        out_shape=[shape] * 4 + [like(a) for a in through],
        input_output_aliases={5 + k: 4 + k for k in range(count)},
        compiler_params=params(8),
        cost_estimate=pl.CostEstimate(flops=1 << 19, bytes_accessed=1 << 20, transcendentals=0),
    )(*parts, dep, *through)


def third_sum_kernel(a, b, c, d, *rest):
    out = rest[len(rest) // 2]
    added = (a[...].astype(F32) + b[...].astype(F32)) + (c[...].astype(F32) + d[...].astype(F32))
    out[0:128, :] = added[0:128]
    out[128:136, :] = 256 * added[128:136] + added[136:144]


def third_sum(parts, *through):
    count = len(through)
    shape = jax.ShapeDtypeStruct((136, 256), F32)
    return pl.pallas_call(
        third_sum_kernel,
        grid=(1,),
        in_specs=[whole(a) for a in parts] + [ANYWHERE] * count,
        out_specs=[whole(shape)] + [ANYWHERE] * count,
        out_shape=[shape] + [like(a) for a in through],
        input_output_aliases={4 + k: 1 + k for k in range(count)},
        compiler_params=params(8),
        cost_estimate=pl.CostEstimate(flops=1 << 17, bytes_accessed=1 << 19, transcendentals=0),
    )(*parts, *through)


def merge_kernel(place, own, other, out, half):
    out[...] = own[...] + other[...]
    rows = pl.ds(pl.multiple_of(place[2] * 64, 64), 64)
    half[...] = own[rows, :] + other[rows, :]


def merge(place, own, other):
    half = jax.ShapeDtypeStruct((64, 256), F32)
    vmem = pl.BlockSpec(memory_space=pltpu.VMEM)
    return pl.pallas_call(
        merge_kernel,
        in_specs=[SMEM] + [vmem] * 2,
        out_specs=[vmem] * 2,
        out_shape=[like(own), half],
        compiler_params=params(8),
        cost_estimate=pl.CostEstimate(flops=1 << 16, bytes_accessed=1 << 19, transcendentals=0),
    )(place, own, other)


def after_kernel(*refs):
    pass


def after(*arrays):
    return pl.pallas_call(
        after_kernel,
        in_specs=[ANYWHERE] * len(arrays),
        out_specs=[ANYWHERE] * len(arrays),
        out_shape=[like(a) for a in arrays],
        input_output_aliases={k: k for k in range(len(arrays))},
        compiler_params=params(8),
        cost_estimate=pl.CostEstimate(flops=0, bytes_accessed=0, transcendentals=0),
    )(*arrays)


def assemble_kernel(place, own, near, near_other, far, *rest):
    x, c = place[0], place[2]
    step = 1 - 2 * c
    out = rest[-1]
    rows = own.shape[0]
    to = (x, lax.rem(x - step + NX, NX), lax.rem(x + step + NX, NX), lax.rem(x + 2, NX))
    for at, part in zip(to, (own, near, near_other, far)):
        out[pl.ds(pl.multiple_of(at * rows, rows), rows), :] = part[...]
    out[NX * rows :, :] = jnp.zeros((PAD, out.shape[1]), BF16)


def assemble(place, parts, dep):
    rows, width = parts[0].shape
    shape = jax.ShapeDtypeStruct((NX * rows + PAD, width), BF16)
    return pl.pallas_call(
        assemble_kernel,
        grid=(1,),
        in_specs=[SMEM] + [whole(a) for a in parts] + [ANYWHERE],
        out_specs=whole(shape),
        out_shape=shape,
        compiler_params=params(8),
        cost_estimate=pl.CostEstimate(flops=0, bytes_accessed=2 << 20, transcendentals=0),
    )(place, *parts, dep)


SPAN = 512


def where_to(place, distance, half):
    block = lax.rem(place[3] + distance * (1 - 2 * place[2]) + NZ, NZ)
    return pl.multiple_of((2 * block + half) * SPAN, SPAN)


def products_kernel(grads, *refs):
    chunks, out = refs[:-1], refs[-1]
    for k, chunk in enumerate(chunks):
        for n in range(2):
            out[2 * k + n] = nt_dot(grads[...], chunk[n * SPAN : (n + 1) * SPAN, :])


def products(grads, chunks):
    tokens, width = grads.shape
    pieces = 2 * len(chunks)
    vmem = pl.BlockSpec(memory_space=pltpu.VMEM)
    return pl.pallas_call(
        products_kernel,
        in_specs=[vmem] * (1 + len(chunks)),
        out_specs=vmem,
        out_shape=jax.ShapeDtypeStruct((pieces, tokens, SPAN), F32),
        compiler_params=params(16),
        cost_estimate=pl.CostEstimate(
            flops=2 * tokens * width * SPAN * pieces, bytes_accessed=pieces << 20, transcendentals=0
        ),
    )(grads, *chunks)


def scale_of(filled, total):
    scale = filled[0:1, :] * (DEVICES / total[128:129, :])
    return jnp.concatenate([scale] * (SPAN // 256), axis=1)


def scaled_kernel(distances, place, filled, total, grads, raw, *refs):
    made, out_sems = refs[-2:]
    chunks, out = refs[:-3], refs[-3]
    count = raw.shape[0]
    scale = scale_of(filled, total)
    stores = []
    for n in range(made.shape[0]):
        if n < count:
            piece = raw[n]
        else:
            k, at = divmod(n - count, 2)
            piece = nt_dot(grads[...], chunks[k][at * SPAN : (at + 1) * SPAN, :])
        made[n] = (piece * scale).astype(BF16)
        to = pl.ds(where_to(place, distances[n // 2], n % 2), SPAN)
        stores.append(pltpu.make_async_copy(made.at[n], out.at[:, to], out_sems.at[n]))
        stores[n].start()
    for store in stores:
        store.wait()


def scaled(place, filled, total, grads, raw, raw_distances, chunks, distances):
    tokens = grads.shape[0]
    count = raw.shape[0] + 2 * len(chunks)
    return pl.pallas_call(
        functools.partial(scaled_kernel, (*raw_distances, *distances)),
        in_specs=[SMEM] + [pl.BlockSpec(memory_space=pltpu.VMEM)] * (4 + len(chunks)),
        out_specs=HBM,
        out_shape=jax.ShapeDtypeStruct((tokens, NZ * NX * 256), BF16),
        scratch_shapes=[
            pltpu.VMEM((count, tokens, SPAN), BF16),
            pltpu.SemaphoreType.DMA((count,)),
        ],
        compiler_params=params(16),
        cost_estimate=pl.CostEstimate(flops=count << 17, bytes_accessed=count * 3 << 18, transcendentals=0),
    )(place, filled, total, grads, raw, *chunks)


def finish_kernel(place, filled, own, near, near_other, far, far_other, grads, last, last_other, *rest):
    weight_out, out, made, done, sems = rest[1:]
    y, c = place[1], place[2]
    step = 1 - 2 * c
    scale = scale_of(filled, own)
    stores = []
    for n, chunk in enumerate((last, last_other)):
        made[n] = (nt_dot(grads[...], chunk[...]) * scale).astype(BF16)
        to = pl.ds(where_to(place, HALF_Z, lax.rem(n + c, 2)), SPAN)
        stores.append(pltpu.make_async_copy(made.at[n], out.at[:, to], sems.at[n]))
        stores[n].start()

    inverse = DEVICES / own[128:129, :]

    def put(feature, part):
        done[:, pl.ds(pl.multiple_of(feature * 128, 128), 128)] = (part * inverse).T

    put(y, own[0:128, :])
    put(lax.rem(y - step + NY, NY), near[0:128, :])
    put(lax.rem(y + step + NY, NY), near_other[0:128, :])
    first = jnp.where(c == 0, far[...], far_other[...])
    second = jnp.where(c == 0, far_other[...], far[...])
    put(lax.rem(y + 2, NY), jnp.concatenate([first, second], axis=0))
    stores.append(pltpu.make_async_copy(done, weight_out, sems.at[2]))
    stores[2].start()
    for store in stores:
        store.wait()


def finish(place, filled, parts, grads, lasts, out):
    shape = jax.ShapeDtypeStruct((256, 512), F32)
    tokens = grads.shape[0]
    operands = [place, filled, *parts, grads, *lasts, out]
    return pl.pallas_call(
        finish_kernel,
        in_specs=[SMEM] + [pl.BlockSpec(memory_space=pltpu.VMEM)] * (len(operands) - 2) + [HBM],
        out_specs=[HBM] * 2,
        out_shape=[shape, like(out)],
        scratch_shapes=[
            pltpu.VMEM((2, tokens, SPAN), BF16),
            pltpu.VMEM(shape.shape, F32),
            pltpu.SemaphoreType.DMA((3,)),
        ],
        input_output_aliases={len(operands) - 1: 1},
        compiler_params=params(8),
        cost_estimate=pl.CostEstimate(flops=1 << 28, bytes_accessed=3 << 20, transcendentals=0),
    )(*operands)


def local(inputs, grad_values, value_weight, counts, loss_mask):
    tok_rows = inputs.shape[0]
    dp, group = lax.axis_index("dp"), lax.axis_index("group")
    z, x, y, c = dp // NX, dp % NX, group // 2, group % 2
    place = jnp.stack([x, y, c, z]).astype(jnp.int32)

    other_x = swap(inputs)
    near = hop(value_weight, lambda z, x, y, c: (z, x + 1 - 2 * c, y, c))
    filled = jnp.full((8, 256), counts[0].astype(F32))
    other_filled = swap(filled)
    positions = jnp.arange(tok_rows, dtype=jnp.int32)
    live = (positions < counts[0]) & (loss_mask > 0)
    grads = jnp.where(live[:, None], grad_values, jnp.zeros_like(grad_values))
    own_t = grads.T
    other_t = swap(own_t)

    rows, width = value_weight.shape
    near_other = swap(near)
    far = hop(near, lambda z, x, y, c: (z, x + 1 - 2 * c, y, c))

    added, grads = own_partials(place, filled, own_t, inputs, grads)
    s0, plus, minus, s1, s3 = partials(place, other_filled, other_t, other_x, added)
    s_moves = lambda r: lambda z, x, y, c: (z, x, y + r, c) if c == 0 else (z, x + r, y, c)
    u_moves = lambda r: lambda z, x, y, c: (z, x + r, y, c) if c == 0 else (z, x, y + r, c)
    around = lambda z, x, y, c: (z + 1 - 2 * c, x, y, c)
    chunk = assemble(place, (value_weight, near, near_other, far), s0)

    ring1 = hop(chunk, around)
    from_minus, from_plus = hop(plus, s_moves(1)), hop(minus, s_moves(-1))
    total = filled + other_filled
    total = total + hop(total, s_moves(1))
    ring1, from_minus, from_plus, total = after(ring1, from_minus, from_plus, total)
    s1, s3 = relay(s1, s3, from_minus, from_plus)

    ring2, ring1_other = hop(ring1, around), swap(ring1)
    late_minus, late_plus = hop(s1, s_moves(1)), hop(s3, s_moves(-1))
    total = total + hop(total, s_moves(2))
    ring2, ring1_other, late_minus, late_plus, total = after(ring2, ring1_other, late_minus, late_plus, total)
    u0, u1, u2, u3 = first_sum(place, total, (s0, from_minus, from_plus, late_minus, late_plus))

    ring3, ring2_other = hop(ring2, around), swap(ring2)
    second = [u0] + [hop(u, u_moves(r)) for r, u in ((1, u1), (2, u2), (3, u3))]
    raw = products(grads, (chunk, ring1, ring1_other, ring2, ring2_other))
    *sends, ring3 = second_sum(second, raw, ring3)

    half = NX * rows // 2
    last = lax.dynamic_slice(ring3, (c * half, 0), (half, width))
    ring3_other = swap(ring3)
    third = [hop(sends[0], lambda z, x, y, c: (z + HALF_Z * c, x, y, c))]
    third += [hop(sends[k], lambda z, x, y, c: (z + k * (1 - 2 * c), x, y, c)) for k in range(1, HALF_Z)]
    block, last, ring3, ring3_other = third_sum(third, last, ring3, ring3_other)

    last = hop(last, around)
    block, part = merge(place, block, swap(block))
    near = hop(block, lambda z, x, y, c: (z, x, y + 1 - 2 * c, c))
    far = hop(part, lambda z, x, y, c: (z, x, y + 2, c))
    input_grad = scaled(place, filled, block, grads, raw, (0, -1, 1, -2, 2), (ring3, ring3_other), (-3, 3))
    near, far, last, input_grad = after(near, far, last, input_grad)
    parts = (block, near, swap(near), far, swap(far))
    weight_grad, input_grad = finish(place, filled, parts, grads, (last, swap(last)), input_grad)
    return (input_grad, weight_grad)


def solution(mesh):
    return jax.shard_map(
        local,
        mesh=mesh,
        in_specs=(
            P(("dp", "group"), None),
            P(("dp", "group"), None),
            P("dp", None),
            P(("dp", "group")),
            P(("dp", "group")),
        ),
        out_specs=(P(("dp", "group"), None), P("dp", None)),
        check_vma=False,
    )
```

```python
import functools

import jax
import jax.numpy as jnp
from jax import lax
from jax.experimental import pallas as pl
from jax.experimental.pallas import tpu as pltpu
from jax.sharding import PartitionSpec as P

NZ, NX, NY = 8, 4, 4
HALF_Z = NZ // 2
DEVICES = NZ * NX * NY * 2
PAD = 16
F32, BF16 = jnp.float32, jnp.bfloat16
MIB = 1 << 20
ANYWHERE = pl.BlockSpec(memory_space=pl.ANY)
HBM = pl.BlockSpec(memory_space=pltpu.HBM)
SMEM = pl.BlockSpec(memory_space=pltpu.SMEM)


def hop(array, move):
    pairs = []
    for z in range(NZ):
        for x in range(NX):
            for y in range(NY):
                for c in range(2):
                    tz, tx, ty, tc = move(z, x, y, c)
                    source = (z * NX + x) * NY * 2 + y * 2 + c
                    target = ((tz % NZ) * NX + tx % NX) * NY * 2 + (ty % NY) * 2 + tc
                    pairs.append((source, target))
    return lax.ppermute(array, ("dp", "group"), pairs)


def swap(array):
    return hop(array, lambda z, x, y, c: (z, x, y, 1 - c))


def nt_dot(left, right):
    return lax.dot_general(left, right, (((1,), (1,)), ((), ())), preferred_element_type=F32)


def nn_dot(left, right):
    return lax.dot_general(left, right, (((1,), (0,)), ((), ())), preferred_element_type=F32)


def params(mib):
    return pltpu.CompilerParams(vmem_limit_bytes=mib * MIB)


def whole(array):
    return pl.BlockSpec(array.shape, lambda *_: (0,) * array.ndim)


def like(array):
    return jax.ShapeDtypeStruct(array.shape, array.dtype)


def turn(place, gradient, out):
    for q in range(NY):
        quarter = lax.select(place[2] == 0, lax.rem(place[1] + q, NY), q)
        out[q * 128 : (q + 1) * 128, :] = gradient[pl.ds(pl.multiple_of(quarter * 128, 128), 128), :]


def step_loads(place, source, held, sems):
    i = pl.program_id(0)
    span = NX * 256

    def load(k):
        far = lax.select(place[2] == 0, jnp.int32(k), jnp.where(k == 0, HALF_Z, NZ - k).astype(jnp.int32))
        cols = pl.ds(pl.multiple_of(lax.rem(place[3] + far, NZ) * span, span), span)
        return pltpu.make_async_copy(source.at[:, cols], held.at[k], sems.at[k])

    @pl.when(i == 0)
    def _():
        load(0).start()
        load(1).start()

    @pl.when((i > 0) & (i < HALF_Z - 1))
    def _():
        load(i + 1).start()

    load(i).wait()


def own_kernel(place, number, gradient, source, grads, added, grads_out, turned, held, sems):
    i = pl.program_id(0)

    @pl.when(i == 0)
    def _():
        turn(place, gradient, turned)

    step_loads(place, source, held, sems)
    for at in range(NX):
        added[i, at] = number[0:1, :] * nn_dot(turned[...], held[i, :, at * 256 : (at + 1) * 256])


def other_kernel(place, number, gradient, source, added, s0, plus, minus, s1, s3, turned, held, sems):
    x, c = place[0], place[2]
    i = pl.program_id(0)

    @pl.when(i == 0)
    def _():
        turn(place, gradient, turned)

    step_loads(place, source, held, sems)

    def store(r, j, tile):
        if r == 0:
            s0[j, i] = tile
            return

        @pl.when(j < 2)
        def _():
            if r == 1:
                s1[j, i] = tile
            elif r == 2:
                plus[j, i] = tile
            else:
                minus[2 + j, i] = tile

        @pl.when(j >= 2)
        def _():
            if r == 1:
                plus[j, i] = tile
            elif r == 2:
                minus[j - 2, i] = tile
            else:
                s3[j - 2, i] = tile

    def product(at):
        cols = pl.ds(pl.multiple_of(at * 256, 256), 256)
        return (added[i, at] + number[0:1, :] * nn_dot(turned[...], held[i, :, cols])).astype(BF16)

    @pl.when(c == 0)
    def _():
        for at in range(NX):
            tile = product(at)
            for q in range(NY):
                store(q, at, tile[q * 128 : (q + 1) * 128])

    @pl.when(c == 1)
    def _():
        for r in range(NX):
            tile = product(lax.rem(x + r, NX))
            for q in range(NY):
                store(r, q, tile[q * 128 : (q + 1) * 128])


def partials_scratch(tokens):
    return [
        pltpu.VMEM((512, tokens), BF16),
        pltpu.VMEM((HALF_Z, tokens, NX * 256), BF16),
        pltpu.SemaphoreType.DMA((HALF_Z,)),
    ]


def own_partials(place, number, gradient, inputs, grads):
    tokens = gradient.shape[1]
    shape = jax.ShapeDtypeStruct((HALF_Z, NX, 512, 256), F32)
    vmem = pl.BlockSpec(memory_space=pltpu.VMEM)
    return pl.pallas_call(
        own_kernel,
        grid=(HALF_Z,),
        in_specs=[SMEM, vmem, vmem, HBM, ANYWHERE],
        out_specs=[vmem, ANYWHERE],
        out_shape=[shape, like(grads)],
        scratch_shapes=partials_scratch(tokens),
        input_output_aliases={4: 1},
        compiler_params=params(16),
        cost_estimate=pl.CostEstimate(flops=512 * 512 * 4096, bytes_accessed=4 << 20, transcendentals=0),
    )(place, number, gradient, inputs, grads)


def partials(place, number, gradient, inputs, added):
    tokens = gradient.shape[1]
    jobs = (4, 4, 4, 2, 2)
    vmem = pl.BlockSpec(memory_space=pltpu.VMEM)
    return pl.pallas_call(
        other_kernel,
        grid=(HALF_Z,),
        in_specs=[SMEM, vmem, vmem, HBM, vmem],
        out_specs=[vmem] * 5,
        out_shape=[jax.ShapeDtypeStruct((j, HALF_Z, 128, 256), BF16) for j in jobs],
        scratch_shapes=partials_scratch(tokens),
        compiler_params=params(16),
        cost_estimate=pl.CostEstimate(flops=512 * 512 * 4096, bytes_accessed=8 << 20, transcendentals=0),
    )(place, number, gradient, inputs, added)


def relay_kernel(s1, s3, from_minus, from_plus, *rest):
    s1_out, s3_out = rest[len(rest) // 2 - 1 : len(rest) // 2 + 1]
    s1_out[...] = (s1[...].astype(F32) + from_minus[...].astype(F32)).astype(BF16)
    s3_out[...] = (s3[...].astype(F32) + from_plus[...].astype(F32)).astype(BF16)


def relay(s1, s3, from_minus, from_plus, *through):
    low = pl.BlockSpec((2, 1, 128, 256), lambda i: (0, i, 0, 0))
    count = len(through)
    return pl.pallas_call(
        relay_kernel,
        grid=(HALF_Z,),
        in_specs=[low] * 4 + [ANYWHERE] * count,
        out_specs=[low] * 2 + [ANYWHERE] * count,
        out_shape=[like(a) for a in (s1, s3, *through)],
        input_output_aliases={0: 0, 1: 1} | {4 + k: 2 + k for k in range(count)},
        compiler_params=params(8),
        cost_estimate=pl.CostEstimate(flops=1 << 20, bytes_accessed=3 << 20, transcendentals=0),
    )(s1, s3, from_minus, from_plus, *through)


def split_count(total):
    high = jnp.floor(total * (1 / 256))
    return jnp.concatenate([high, total - 256 * high], axis=0)


def first_sum_kernel(place, total, s0, from_minus, from_plus, late_minus, late_plus, u0, u1, u2, u3, added):
    i = pl.program_id(0)
    for k in range(2):
        added[k] = s0[k, 0].astype(F32) + (late_minus[k, 0].astype(F32) + from_plus[k, 0].astype(F32))
        added[2 + k] = s0[2 + k, 0].astype(F32) + (late_plus[k, 0].astype(F32) + from_minus[k, 0].astype(F32))
    own = lax.select(place[2] == 0, place[0], place[1])
    rows = pl.ds(pl.multiple_of(i * 128, 128), 128)
    for r, u in enumerate((u0, u1, u2, u3)):
        u[rows, :] = added[lax.rem(own + r, 4)].astype(u.dtype)

    @pl.when(i == 0)
    def _():
        ends = split_count(total[...])
        for u in (u0, u1, u2, u3):
            u[HALF_Z * 128 :, :] = ends.astype(u.dtype)


def first_sum(place, total, parts):
    four = pl.BlockSpec((4, 1, 128, 256), lambda i: (0, i, 0, 0))
    low = pl.BlockSpec((2, 1, 128, 256), lambda i: (0, i, 0, 0))
    high = pl.BlockSpec((2, 1, 128, 256), lambda i: (1, i, 0, 0))
    vmem = pl.BlockSpec(memory_space=pltpu.VMEM)
    shape = (HALF_Z * 128 + 16, 256)
    return pl.pallas_call(
        first_sum_kernel,
        grid=(HALF_Z,),
        in_specs=[SMEM, vmem, four, high, high, low, low],
        out_specs=[vmem] * 4,
        out_shape=[jax.ShapeDtypeStruct(shape, F32)] + [jax.ShapeDtypeStruct(shape, BF16)] * 3,
        scratch_shapes=[pltpu.VMEM((4, 128, 256), F32)],
        compiler_params=params(8),
        cost_estimate=pl.CostEstimate(flops=1 << 20, bytes_accessed=4 << 20, transcendentals=0),
    )(place, total, *parts)


def second_sum_kernel(a, b, c, d, dep, *rest):
    count = (len(rest) - 4) // 2
    ends = HALF_Z * 128

    def added(rows):
        return (a[rows, :] + b[rows, :].astype(F32)) + (c[rows, :].astype(F32) + d[rows, :].astype(F32))

    counts = added(slice(ends, ends + 16))
    counts = split_count(256 * counts[0:8] + counts[8:16])
    for k, v in enumerate(rest[count : count + 4]):
        v[0:128, :] = added(slice(k * 128, (k + 1) * 128)).astype(v.dtype)
        v[128:144, :] = counts.astype(v.dtype)


def second_sum(parts, dep, *through):
    count = len(through)
    shape = jax.ShapeDtypeStruct((144, 256), BF16)
    return pl.pallas_call(
        second_sum_kernel,
        grid=(1,),
        in_specs=[whole(a) for a in parts] + [ANYWHERE] * (1 + count),
        out_specs=[whole(shape)] * 4 + [ANYWHERE] * count,
        out_shape=[shape] * 4 + [like(a) for a in through],
        input_output_aliases={5 + k: 4 + k for k in range(count)},
        compiler_params=params(8),
        cost_estimate=pl.CostEstimate(flops=1 << 19, bytes_accessed=1 << 20, transcendentals=0),
    )(*parts, dep, *through)


def third_sum_kernel(a, b, c, d, *rest):
    out = rest[len(rest) // 2]
    added = (a[...].astype(F32) + b[...].astype(F32)) + (c[...].astype(F32) + d[...].astype(F32))
    out[0:128, :] = added[0:128]
    out[128:136, :] = 256 * added[128:136] + added[136:144]


def third_sum(parts, *through):
    count = len(through)
    shape = jax.ShapeDtypeStruct((136, 256), F32)
    return pl.pallas_call(
        third_sum_kernel,
        grid=(1,),
        in_specs=[whole(a) for a in parts] + [ANYWHERE] * count,
        out_specs=[whole(shape)] + [ANYWHERE] * count,
        out_shape=[shape] + [like(a) for a in through],
        input_output_aliases={4 + k: 1 + k for k in range(count)},
        compiler_params=params(8),
        cost_estimate=pl.CostEstimate(flops=1 << 17, bytes_accessed=1 << 19, transcendentals=0),
    )(*parts, *through)


def merge_kernel(place, own, other, out, half):
    out[...] = own[...] + other[...]
    rows = pl.ds(pl.multiple_of(place[2] * 64, 64), 64)
    half[...] = own[rows, :] + other[rows, :]


def merge(place, own, other):
    half = jax.ShapeDtypeStruct((64, 256), F32)
    vmem = pl.BlockSpec(memory_space=pltpu.VMEM)
    return pl.pallas_call(
        merge_kernel,
        in_specs=[SMEM] + [vmem] * 2,
        out_specs=[vmem] * 2,
        out_shape=[like(own), half],
        compiler_params=params(8),
        cost_estimate=pl.CostEstimate(flops=1 << 16, bytes_accessed=1 << 19, transcendentals=0),
    )(place, own, other)


def after_kernel(*refs):
    pass


def after(*arrays):
    return pl.pallas_call(
        after_kernel,
        in_specs=[ANYWHERE] * len(arrays),
        out_specs=[ANYWHERE] * len(arrays),
        out_shape=[like(a) for a in arrays],
        input_output_aliases={k: k for k in range(len(arrays))},
        compiler_params=params(8),
        cost_estimate=pl.CostEstimate(flops=0, bytes_accessed=0, transcendentals=0),
    )(*arrays)


def assemble_kernel(place, own, near, near_other, far, *rest):
    x, c = place[0], place[2]
    step = 1 - 2 * c
    out = rest[-1]
    rows = own.shape[0]
    to = (x, lax.rem(x - step + NX, NX), lax.rem(x + step + NX, NX), lax.rem(x + 2, NX))
    for at, part in zip(to, (own, near, near_other, far)):
        out[pl.ds(pl.multiple_of(at * rows, rows), rows), :] = part[...]
    out[NX * rows :, :] = jnp.zeros((PAD, out.shape[1]), BF16)


def assemble(place, parts, dep):
    rows, width = parts[0].shape
    shape = jax.ShapeDtypeStruct((NX * rows + PAD, width), BF16)
    return pl.pallas_call(
        assemble_kernel,
        grid=(1,),
        in_specs=[SMEM] + [whole(a) for a in parts] + [ANYWHERE],
        out_specs=whole(shape),
        out_shape=shape,
        compiler_params=params(8),
        cost_estimate=pl.CostEstimate(flops=0, bytes_accessed=2 << 20, transcendentals=0),
    )(place, *parts, dep)


SPAN = 512


def where_to(place, distance, half):
    block = lax.rem(place[3] + distance * (1 - 2 * place[2]) + NZ, NZ)
    return pl.multiple_of((2 * block + half) * SPAN, SPAN)


def products_kernel(grads, *refs):
    chunks, out = refs[:-1], refs[-1]
    for k, chunk in enumerate(chunks):
        for n in range(2):
            out[2 * k + n] = nt_dot(grads[...], chunk[n * SPAN : (n + 1) * SPAN, :]).astype(BF16)


def products(grads, chunks):
    tokens, width = grads.shape
    pieces = 2 * len(chunks)
    vmem = pl.BlockSpec(memory_space=pltpu.VMEM)
    return pl.pallas_call(
        products_kernel,
        in_specs=[vmem] * (1 + len(chunks)),
        out_specs=vmem,
        out_shape=jax.ShapeDtypeStruct((pieces, tokens, SPAN), BF16),
        compiler_params=params(16),
        cost_estimate=pl.CostEstimate(
            flops=2 * tokens * width * SPAN * pieces, bytes_accessed=pieces * 3 << 18, transcendentals=0
        ),
    )(grads, *chunks)


def scale_of(filled, total):
    scale = filled[0:1, :] * (DEVICES / total[128:129, :])
    return jnp.concatenate([scale] * (SPAN // 256), axis=1)


def scaled_kernel(distances, place, filled, total, grads, raw, *refs):
    made, out_sems = refs[-2:]
    chunks, out = refs[:-3], refs[-3]
    count = raw.shape[0]
    scale = scale_of(filled, total)
    stores = []
    for n in range(made.shape[0]):
        if n < count:
            piece = raw[n].astype(F32)
        else:
            k, at = divmod(n - count, 2)
            piece = nt_dot(grads[...], chunks[k][at * SPAN : (at + 1) * SPAN, :])
        made[n] = (piece * scale).astype(BF16)
        to = pl.ds(where_to(place, distances[n // 2], n % 2), SPAN)
        stores.append(pltpu.make_async_copy(made.at[n], out.at[:, to], out_sems.at[n]))
        stores[n].start()
    for store in stores:
        store.wait()


def scaled(place, filled, total, grads, raw, raw_distances, chunks, distances):
    tokens = grads.shape[0]
    count = raw.shape[0] + 2 * len(chunks)
    return pl.pallas_call(
        functools.partial(scaled_kernel, (*raw_distances, *distances)),
        in_specs=[SMEM] + [pl.BlockSpec(memory_space=pltpu.VMEM)] * (4 + len(chunks)),
        out_specs=HBM,
        out_shape=jax.ShapeDtypeStruct((tokens, NZ * NX * 256), BF16),
        scratch_shapes=[
            pltpu.VMEM((count, tokens, SPAN), BF16),
            pltpu.SemaphoreType.DMA((count,)),
        ],
        compiler_params=params(16),
        cost_estimate=pl.CostEstimate(flops=count << 17, bytes_accessed=count * 3 << 18, transcendentals=0),
    )(place, filled, total, grads, raw, *chunks)


def finish_kernel(place, filled, own, near, near_other, far, far_other, grads, last, last_other, *rest):
    weight_out, out, made, done, sems = rest[1:]
    y, c = place[1], place[2]
    step = 1 - 2 * c
    scale = scale_of(filled, own)
    stores = []
    for n, chunk in enumerate((last, last_other)):
        made[n] = (nt_dot(grads[...], chunk[...]) * scale).astype(BF16)
        to = pl.ds(where_to(place, HALF_Z, lax.rem(n + c, 2)), SPAN)
        stores.append(pltpu.make_async_copy(made.at[n], out.at[:, to], sems.at[n]))
        stores[n].start()

    inverse = DEVICES / own[128:129, :]

    def put(feature, part):
        done[:, pl.ds(pl.multiple_of(feature * 128, 128), 128)] = (part * inverse).T

    put(y, own[0:128, :])
    put(lax.rem(y - step + NY, NY), near[0:128, :])
    put(lax.rem(y + step + NY, NY), near_other[0:128, :])
    first = jnp.where(c == 0, far[...], far_other[...])
    second = jnp.where(c == 0, far_other[...], far[...])
    put(lax.rem(y + 2, NY), jnp.concatenate([first, second], axis=0))
    stores.append(pltpu.make_async_copy(done, weight_out, sems.at[2]))
    stores[2].start()
    for store in stores:
        store.wait()


def finish(place, filled, parts, grads, lasts, out):
    shape = jax.ShapeDtypeStruct((256, 512), F32)
    tokens = grads.shape[0]
    operands = [place, filled, *parts, grads, *lasts, out]
    return pl.pallas_call(
        finish_kernel,
        in_specs=[SMEM] + [pl.BlockSpec(memory_space=pltpu.VMEM)] * (len(operands) - 2) + [HBM],
        out_specs=[HBM] * 2,
        out_shape=[shape, like(out)],
        scratch_shapes=[
            pltpu.VMEM((2, tokens, SPAN), BF16),
            pltpu.VMEM(shape.shape, F32),
            pltpu.SemaphoreType.DMA((3,)),
        ],
        input_output_aliases={len(operands) - 1: 1},
        compiler_params=params(8),
        cost_estimate=pl.CostEstimate(flops=1 << 28, bytes_accessed=3 << 20, transcendentals=0),
    )(*operands)


def local(inputs, grad_values, value_weight, counts, loss_mask):
    tok_rows = inputs.shape[0]
    dp, group = lax.axis_index("dp"), lax.axis_index("group")
    z, x, y, c = dp // NX, dp % NX, group // 2, group % 2
    place = jnp.stack([x, y, c, z]).astype(jnp.int32)

    other_x = swap(inputs)
    near = hop(value_weight, lambda z, x, y, c: (z, x + 1 - 2 * c, y, c))
    filled = jnp.full((8, 256), counts[0].astype(F32))
    other_filled = swap(filled)
    positions = jnp.arange(tok_rows, dtype=jnp.int32)
    live = (positions < counts[0]) & (loss_mask > 0)
    grads = jnp.where(live[:, None], grad_values, jnp.zeros_like(grad_values))
    own_t = grads.T
    other_t = swap(own_t)

    rows, width = value_weight.shape
    near_other = swap(near)
    far = hop(near, lambda z, x, y, c: (z, x + 1 - 2 * c, y, c))

    added, grads = own_partials(place, filled, own_t, inputs, grads)
    s0, plus, minus, s1, s3 = partials(place, other_filled, other_t, other_x, added)
    s_moves = lambda r: lambda z, x, y, c: (z, x, y + r, c) if c == 0 else (z, x + r, y, c)
    u_moves = lambda r: lambda z, x, y, c: (z, x + r, y, c) if c == 0 else (z, x, y + r, c)
    around = lambda z, x, y, c: (z + 1 - 2 * c, x, y, c)
    chunk = assemble(place, (value_weight, near, near_other, far), s0)

    ring1 = hop(chunk, around)
    from_minus, from_plus = hop(plus, s_moves(1)), hop(minus, s_moves(-1))
    total = filled + other_filled
    total = total + hop(total, s_moves(1))
    ring1, from_minus, from_plus, total = after(ring1, from_minus, from_plus, total)
    s1, s3 = relay(s1, s3, from_minus, from_plus)

    ring2, ring1_other = hop(ring1, around), swap(ring1)
    late_minus, late_plus = hop(s1, s_moves(1)), hop(s3, s_moves(-1))
    total = total + hop(total, s_moves(2))
    ring2, ring1_other, late_minus, late_plus, total = after(ring2, ring1_other, late_minus, late_plus, total)
    u0, u1, u2, u3 = first_sum(place, total, (s0, from_minus, from_plus, late_minus, late_plus))

    ring3, ring2_other = hop(ring2, around), swap(ring2)
    second = [u0] + [hop(u, u_moves(r)) for r, u in ((1, u1), (2, u2), (3, u3))]
    raw = products(grads, (chunk, ring1, ring1_other, ring2, ring2_other))
    *sends, ring3 = second_sum(second, raw, ring3)

    half = NX * rows // 2
    last = lax.dynamic_slice(ring3, (c * half, 0), (half, width))
    ring3_other = swap(ring3)
    third = [hop(sends[0], lambda z, x, y, c: (z + HALF_Z * c, x, y, c))]
    third += [hop(sends[k], lambda z, x, y, c: (z + k * (1 - 2 * c), x, y, c)) for k in range(1, HALF_Z)]
    block, last, ring3, ring3_other = third_sum(third, last, ring3, ring3_other)

    last = hop(last, around)
    block, part = merge(place, block, swap(block))
    near = hop(block, lambda z, x, y, c: (z, x, y + 1 - 2 * c, c))
    far = hop(part, lambda z, x, y, c: (z, x, y + 2, c))
    input_grad = scaled(place, filled, block, grads, raw, (0, -1, 1, -2, 2), (ring3, ring3_other), (-3, 3))
    near, far, last, input_grad = after(near, far, last, input_grad)
    parts = (block, near, swap(near), far, swap(far))
    weight_grad, input_grad = finish(place, filled, parts, grads, (last, swap(last)), input_grad)
    return (input_grad, weight_grad)


def solution(mesh):
    return jax.shard_map(
        local,
        mesh=mesh,
        in_specs=(
            P(("dp", "group"), None),
            P(("dp", "group"), None),
            P("dp", None),
            P(("dp", "group")),
            P(("dp", "group")),
        ),
        out_specs=(P(("dp", "group"), None), P("dp", None)),
        check_vma=False,
    )
```
